32 devices in a mesh: obs: 4 (over y, x), tm: 8 (over z, core).
Axes of the slice: x: 2, y: 2, z: 4, core: 2. Of those that a mesh axis runs over, the one named last changes fastest.
Arguments:
- flow: float32 [5, 512, 2048], P(None, 'tm', 'obs'), may hold values from -6 to 6
- point_pos: float32 [3, 2048], P(None, 'obs'), may hold values from -1 to 1
- area_vec: float32 [3, 2048], P(None, 'obs'), may hold values from -6.363961 to 6.363961
- observer_angles: float32 [2, 512], P(None, 'obs'), may hold values from -3.140625 to 3.140625
- band_offset: int32 [4, 4], replicated, may hold values from 0 to 61, as said below
Outputs:
- pressure: float32 [512, 512], P('tm', 'obs')
The draws below stay inside these ranges and needn't reach their ends.
Inputs may be any that keep to these rules, and one draw needn't show every extreme that they name: band_offset[g, b] is the whole number of time steps added to every delay from point block b to observer group g; both 0 and 61 occur.
All inputs are finite; a program needn't handle non-finite values.
Results may differ from the reference program's by a relative error of at most 0.0041.
Values may be sent and summed in bfloat16 or wider, within the bound.
A program may use at most 64 MiB of HBM per device.

```python
import math
import jax
import jax.numpy as jnp
from jax import lax

PTS_DEV = 512
GROUP_OBS = 128
BLOCK = 64
LAGS = 4
GROUPS = 4
OBSERVERS = 512
POINTS = 2048
STEPS = 512
MAX_DELAY = 61


def draw_band_offset(key, part):
    entries = GROUPS * GROUPS
    key_values, key_first, key_second = jax.random.split(key, 3)
    values = jax.random.randint(key_values, (entries,), 0, MAX_DELAY + 1)
    first_slot = jax.random.randint(key_first, (), 0, entries)
    second_slot = (first_slot + 1 + jax.random.randint(key_second, (), 0, entries - 1)) % entries
    position = jnp.arange(entries)
    values = jnp.where(position == first_slot, MAX_DELAY, values)
    values = jnp.where(position == second_slot, 0, values)
    return values.reshape(GROUPS, GROUPS).astype(jnp.int32)


def block_scale(own_key, dims, shards, least, high):
    def one(dim, parts):
        heights = jax.random.uniform(jax.random.fold_in(jax.random.fold_in(own_key, 6), dim), (parts,), jnp.float32, least / len(shards), high / len(shards))
        return jnp.repeat(jnp.exp(heights), dims[dim] // parts).reshape((-1,) + (1,) * (len(dims) - dim - 1))

    gain = one(*shards[0])
    for cut in shards[1:]:
        gain = gain * one(*cut)
    return gain


def noise(key, extent, spread, most, pieces=(), kind=jnp.bfloat16):
    factor_of = block_scale(key, extent, pieces, -0.22, 0.18) if pieces else 1.0
    array = jax.random.normal(key, extent, jnp.float32) * spread * factor_of
    return jnp.minimum(jnp.maximum(array, -most), most).astype(kind)


def setup_inputs(seed: int = 0) -> dict:
    key_list = jax.random.split(jax.random.key(seed), 6)
    flow = noise(key_list[0], (5, STEPS, POINTS), 1.0, 6.0, ((1, 8), (2, 4)), jnp.float32)
    point_pos = jnp.clip(jax.random.uniform(key_list[1], (3, POINTS), jnp.float32, -1.0, 1.0) * block_scale(key_list[1], (3, POINTS), ((1, 4),), -0.4, 0.0), -1.0, 1.0)
    area_vec = noise(key_list[2], (3, POINTS), (48.0 / POINTS ** 0.5), 6.363961, ((1, 4),), jnp.float32)
    observer_angles = jnp.clip(jax.random.uniform(key_list[3], (2, OBSERVERS), jnp.float32, -3.140625, 3.140625), -3.140625, 3.140625)
    band_offset = draw_band_offset(jax.random.fold_in(key_list[5], 71), 0)
    return dict(flow=flow, point_pos=point_pos, area_vec=area_vec, observer_angles=observer_angles, band_offset=band_offset)


FOUR_PI_INV = 1.0 / (4.0 * math.pi)
NEAR_RANGE = 3.25
SOUND_STEP = 1.17
SPHERE_RADIUS = 5.0

def observer_xyz(angles):
    azimuth = angles[0]
    elevation = angles[1]
    return SPHERE_RADIUS * jnp.stack([jnp.cos(azimuth) * jnp.cos(elevation), jnp.sin(azimuth) * jnp.cos(elevation), jnp.sin(elevation)])

def source_terms(rimmed, area_vec):
    density = 1.0 + 0.2 * rimmed[0]
    velocity = 0.4 * rimmed[1:4]
    pressure = rimmed[4]
    normal_flux = lax.optimization_barrier(jnp.sum(velocity * area_vec[:, None, :], axis=0))
    mass_flux = density * normal_flux
    loading = pressure[None] * area_vec[:, None, :] + density[None] * velocity * normal_flux[None]
    stacked = jnp.concatenate([mass_flux[None], loading], axis=0)
    rate_terms = 0.5 * (stacked[:, 2:] - stacked[:, :-2])
    return jnp.concatenate([rate_terms, loading[:, 1:-1]], axis=0).astype(jnp.bfloat16)

def pair_weights(observers, points, lag_count):
    separation = observers[:, None, :] - points[:, :, None]
    distance = jnp.sqrt(lax.optimization_barrier(jnp.sum(separation * separation, axis=0)))
    inverse = 1.0 / distance
    direction = separation * inverse[None]
    lag_steps = (distance - NEAR_RANGE) / SOUND_STEP
    shifts = jnp.arange(lag_count).astype(distance.dtype)
    tent_weights = jnp.maximum(0.0, 1.0 - jnp.abs(shifts[None, :, None] - lag_steps[:, None, :]))
    coeffs = jnp.concatenate([inverse[None], direction * (inverse / SOUND_STEP)[None], direction * (inverse * inverse)[None]], axis=0) * FOUR_PI_INV
    return (coeffs[:, :, None, :] * tent_weights[None]).astype(jnp.bfloat16)

def placed_whole(shard_terms, weights, offset, buffer_len):
    product = jnp.einsum('kts,kswo->two', shard_terms.astype(jnp.float32), weights.astype(jnp.float32))
    lag_count = product.shape[1]
    combined = jnp.pad(product[:, 0], ((0, lag_count - 1), (0, 0)))
    for lag_index in range(1, lag_count):
        combined = combined + jnp.pad(product[:, lag_index], ((lag_index, lag_count - 1 - lag_index), (0, 0)))
    canvas = jnp.zeros((buffer_len, product.shape[2]), jnp.float32)
    return lax.dynamic_update_slice(canvas, combined, (offset.astype(jnp.int32), jnp.zeros((), jnp.int32)))

def reference(flow, point_pos, area_vec, observer_angles, band_offset):
    padded = jnp.pad(flow, ((0, 0), (1, 1), (0, 0)))
    all_terms = source_terms(padded, area_vec)
    places = observer_xyz(observer_angles)

    def one_group(group_index):
        group_places = lax.dynamic_slice_in_dim(places, group_index * GROUP_OBS, GROUP_OBS, 1)

        def one_block(accumulated, block_index):
            shard_points = lax.dynamic_slice_in_dim(point_pos, block_index * PTS_DEV, PTS_DEV, 1)
            shard_terms = lax.dynamic_slice_in_dim(all_terms, block_index * PTS_DEV, PTS_DEV, 2)
            weights = pair_weights(group_places, shard_points, LAGS)
            return (accumulated + placed_whole(shard_terms, weights, band_offset[group_index, block_index], STEPS + BLOCK), None)
        initial = jnp.zeros((STEPS + BLOCK, GROUP_OBS), jnp.float32)
        accumulated, unused = lax.scan(one_block, initial, jnp.arange(GROUPS, dtype=jnp.int32))
        return accumulated[:STEPS]
    per_group = lax.map(one_group, jnp.arange(GROUPS, dtype=jnp.int32))
    return jnp.transpose(per_group, (1, 0, 2)).reshape(STEPS, OBSERVERS)
```

```python
import functools
import math

import jax
import jax.numpy as jnp
from jax import lax
from jax.experimental import pallas as pl
from jax.experimental.pallas import tpu as pltpu
from jax.sharding import PartitionSpec as P

LAGS = 4
FOUR_PI = 4.0 * math.pi
NEAR_RANGE = 3.25
SOUND_STEP = 1.17
SPHERE_RADIUS = 5.0
MESH = pl.DeviceIdType.MESH
F32 = jnp.float32
BF16 = jnp.bfloat16
TAIL = 8
CHUNK = 64


def split3(x):
    high = x.astype(BF16).astype(F32)
    rest = x - high
    mid = rest.astype(BF16).astype(F32)
    low = (rest - mid).astype(BF16).astype(F32)
    return high, mid, low


def squares(x):
    return x[0:1] * x[0:1] + x[1:2] * x[1:2] + x[2:3] * x[2:3]


def point_factors(points):
    scaled = FOUR_PI * points
    high, mid, low = split3(scaled)
    s_high, s_mid, s_low = split3(squares(scaled))
    ones = jnp.ones((3, points.shape[1]), F32)
    pad = jnp.zeros((8, points.shape[1]), F32)
    rows = [high, high, mid, high, low, mid, s_high, s_mid, s_low, ones, pad]
    return jnp.concatenate(rows, axis=0)


def observer_factors(places):
    scaled = FOUR_PI * places
    high, mid, low = split3(-2.0 * scaled)
    s_high, s_mid, s_low = split3(squares(scaled))
    ones = jnp.ones((3, places.shape[1]), F32)
    pad = jnp.zeros((8, places.shape[1]), F32)
    rows = [high, mid, high, low, high, mid, ones, s_high, s_mid, s_low, pad]
    return jnp.concatenate(rows, axis=0)


def fluxes(flow, area):
    density = 1.0 + 0.2 * flow[0]
    velocity = [0.4 * flow[1 + i] for i in range(3)]
    normal = velocity[0] * area[0:1] + velocity[1] * area[1:2] + velocity[2] * area[2:3]
    mass = density * normal
    return [mass] + [flow[4] * area[i : i + 1] + density * velocity[i] * normal for i in range(3)]


def kernel(
    groups, blocks,
    flow_hbm, pos_hbm, area_hbm, angles_hbm, band_hbm, out_ref,
    flow, pos, area, angles, band, places, edge_out, edge_in, flux, steady_rate, mass_rate,
    w_mass, w_load, sent, landed,
    in_sem, place_send, place_recv, edge_send, edge_recv, part_send, part_recv,
):
    me = lax.axis_index("obs")
    now = lax.axis_index("tm")
    steps = flow.shape[1]
    points = flow.shape[2]
    has_before = now > 0
    has_after = now < blocks - 1

    barrier = pltpu.get_barrier_semaphore()

    def greet(group, block):
        pl.semaphore_signal(barrier, inc=1, device_id=(group, block), device_id_type=MESH)

    for i in range(1, groups):
        greet(lax.rem(me + i, groups), now)

    @pl.when(has_before)
    def _():
        for i in range(groups):
            greet(lax.rem(me + i, groups), now - 1)

    @pl.when(has_after)
    def _():
        for i in range(groups):
            greet(lax.rem(me + i, groups), now + 1)

    loads = [
        pltpu.make_async_copy(source, target, in_sem.at[i])
        for i, (source, target) in enumerate(
            [(angles_hbm, angles), (flow_hbm, flow), (area_hbm, area), (pos_hbm, pos), (band_hbm, band)]
        )
    ]
    for load in loads:
        load.start()

    loads[0].wait()
    azimuth = angles[0:1, :]
    elevation = angles[1:2, :]
    cos_e = jnp.cos(elevation)
    width = azimuth.shape[1]
    places[me] = jnp.concatenate(
        [
            SPHERE_RADIUS * (jnp.cos(azimuth) * cos_e),
            SPHERE_RADIUS * (jnp.sin(azimuth) * cos_e),
            SPHERE_RADIUS * jnp.sin(elevation),
            jnp.zeros((5, width), F32),
        ],
        axis=0,
    )

    loads[1].wait()
    loads[2].wait()
    area_rows = area[...]
    whole = fluxes(flow, area_rows)
    for k in range(4):
        flux[k] = whole[k]
    edge_pad = jnp.zeros((4, points), F32)
    edge_out[0] = jnp.concatenate([flux[k, 0:1, :] for k in range(4)] + [edge_pad], axis=0)
    edge_out[1] = jnp.concatenate(
        [flux[k, steps - 1 : steps, :] for k in range(4)] + [edge_pad], axis=0
    )

    neighbours = jnp.minimum(now, 1) + jnp.minimum(blocks - 1 - now, 1)
    pl.semaphore_wait(barrier, groups - 1 + groups * neighbours)

    def place_copy(i):
        return pltpu.make_async_remote_copy(
            src_ref=places.at[me], dst_ref=places.at[me],
            send_sem=place_send.at[i], recv_sem=place_recv.at[me],
            device_id=(lax.rem(me + i, groups), now), device_id_type=MESH,
        )

    def edge_copy(side, block):
        return pltpu.make_async_remote_copy(
            src_ref=edge_out.at[side], dst_ref=edge_in.at[side],
            send_sem=edge_send.at[side], recv_sem=edge_recv.at[side],
            device_id=(me, block), device_id_type=MESH,
        )

    for i in range(1, groups):
        place_copy(i).start()

    @pl.when(has_before)
    def _():
        edge_copy(0, now - 1).start()

    @pl.when(has_after)
    def _():
        edge_copy(1, now + 1).start()

    for j in range(2):
        for b in range(groups):
            landed[j, b, 0:steps, :] = jnp.zeros((steps, width), F32)
            landed[j, b, 2 * steps + TAIL :, :] = jnp.zeros((steps - TAIL, width), F32)

    loads[3].wait()
    loads[4].wait()
    spots = pos[...]
    factors = jnp.transpose(point_factors(spots)).astype(BF16)
    spot_rows = [spots[i : i + 1, :] for i in range(3)]

    def with_projection(parts):
        rounded = [part.astype(BF16) for part in parts]
        wide = [part.astype(F32) for part in rounded]
        along = wide[0] * spot_rows[0] + wide[1] * spot_rows[1] + wide[2] * spot_rows[2]
        return jnp.concatenate(rounded + [(-along).astype(BF16)], axis=0)

    steady_rate[:, points:] = with_projection([flux[1 + k] for k in range(3)])

    @pl.when(has_before)
    def _():
        edge_copy(1, now - 1).wait_recv()

    @pl.when(has_after)
    def _():
        edge_copy(0, now + 1).wait_recv()

    @pl.when(jnp.logical_not(has_before))
    def _():
        edge_in[1] = jnp.zeros((8, points), F32)

    @pl.when(jnp.logical_not(has_after))
    def _():
        edge_in[0] = jnp.zeros((8, points), F32)

    row = lax.broadcasted_iota(jnp.int32, (steps, points), 0)
    rates = []
    for k in range(4):
        mine = flux[k]
        later = jnp.where(row == steps - 1, edge_in[0, k : k + 1, :], pltpu.roll(mine, steps - 1, 0))
        earlier = jnp.where(row == 0, edge_in[1, k : k + 1, :], pltpu.roll(mine, 1, 0))
        rates.append(0.5 * (later - earlier))
    mass_rate[...] = rates[0].astype(BF16)
    steady_rate[:, :points] = with_projection(rates[1:])

    near = 1.0 / (SOUND_STEP * FOUR_PI)
    slope = NEAR_RANGE / SOUND_STEP

    def weigh(slot, group_places):
        squared = jnp.dot(
            factors, observer_factors(group_places).astype(BF16), preferred_element_type=F32
        )
        for start in range(0, points, CHUNK):
            rows = slice(start, start + CHUNK)
            load_rows = slice(points + start, points + start + CHUNK)
            r = lax.rsqrt(squared[rows])
            u = near - slope * r
            z = u - r
            y = z - r
            tents = [
                jnp.maximum(0.0, -z),
                jnp.maximum(0.0, jnp.minimum(u, -y)),
                jnp.maximum(0.0, jnp.minimum(z, r - y)),
                jnp.maximum(0.0, y),
            ]
            by_rate = r * (FOUR_PI / SOUND_STEP)
            by_load = r * r * (FOUR_PI * FOUR_PI)
            for j in range(LAGS):
                columns = slice(j * width, (j + 1) * width)
                w_mass[slot, rows, columns] = tents[j].astype(BF16)
                w_load[slot, rows, columns] = (tents[j] * by_rate).astype(BF16)
                w_load[slot, load_rows, columns] = (tents[j] * by_load).astype(BF16)

    def part_copy(i, group, later):
        return pltpu.make_async_remote_copy(
            src_ref=sent.at[group], dst_ref=landed.at[later, me, pl.ds(steps, steps + TAIL), :],
            send_sem=part_send.at[later, i], recv_sem=part_recv.at[later, me],
            device_id=(group, now + later), device_id_type=MESH,
        )

    for i in range(groups):
        group = lax.rem(me + i, groups)
        if i > 0:
            pltpu.make_async_remote_copy(
                src_ref=places.at[group], dst_ref=places.at[group],
                send_sem=place_send.at[i], recv_sem=place_recv.at[group],
                device_id=(group, now), device_id_type=MESH,
            ).wait_recv()
        slot = i % 2
        group_places = places[group][0:3]
        weigh(slot, group_places)
        by_mass = jnp.dot(mass_rate[...], w_mass[slot], preferred_element_type=F32)
        by_load = jnp.dot(steady_rate[...], w_load[slot], preferred_element_type=F32)
        total = jnp.zeros((steps + TAIL, width), F32)
        for j in range(LAGS):
            columns = slice(j * width, (j + 1) * width)
            piece = by_mass[:, columns] + by_load[3 * steps :, columns]
            for k in range(3):
                piece = piece + by_load[k * steps : (k + 1) * steps, columns] * group_places[k : k + 1]
            piece = jnp.concatenate([piece, jnp.zeros((TAIL, width), F32)], axis=0)
            total = total + (pltpu.roll(piece, j, 0) if j else piece)
        sent[group] = total
        if i > 0:
            part_copy(i, group, 0).start()
        else:
            landed[0, me, steps : 2 * steps + TAIL, :] = total

        @pl.when(has_after)
        def _():
            part_copy(i, group, 1).start()

    def arrived(later, block):
        return pltpu.make_async_remote_copy(
            src_ref=sent.at[0], dst_ref=landed.at[later, block, pl.ds(steps, steps + TAIL), :],
            send_sem=part_send.at[later, 0], recv_sem=part_recv.at[later, block],
            device_id=(lax.rem(me + 1, groups), now), device_id_type=MESH,
        )

    for i in range(1, groups):
        arrived(0, lax.rem(me + i, groups)).wait_recv()

    @pl.when(has_before)
    def _():
        for b in range(groups):
            arrived(1, b).wait_recv()

    @pl.when(jnp.logical_not(has_before))
    def _():
        for b in range(groups):
            landed[1, b, steps : 2 * steps + TAIL, :] = jnp.zeros((steps + TAIL, width), F32)

    result = jnp.zeros((steps, width), F32)
    for b in range(groups):
        offset = band[me, b]
        result = result + landed[0, b, pl.ds(steps - offset, steps), :]
        result = result + landed[1, b, pl.ds(2 * steps - offset, steps), :]
    out_ref[...] = result

    for i in range(1, groups):
        place_copy(i).wait_send()
        part_copy(i, lax.rem(me + i, groups), 0).wait_send()

    @pl.when(has_before)
    def _():
        edge_copy(0, now - 1).wait_send()

    @pl.when(has_after)
    def _():
        edge_copy(1, now + 1).wait_send()
        for i in range(groups):
            part_copy(i, lax.rem(me + i, groups), 1).wait_send()


def solution(mesh):
    groups = mesh.shape["obs"]
    blocks = mesh.shape["tm"]

    def local(flow, point_pos, area_vec, observer_angles, band_offset):
        steps, points = flow.shape[1:]
        width = observer_angles.shape[1]
        any_spec = pl.BlockSpec(memory_space=pl.ANY)
        dma = pltpu.SemaphoreType.DMA
        return pl.pallas_call(
            functools.partial(kernel, groups, blocks),
            out_shape=jax.ShapeDtypeStruct((steps, width), F32),
            in_specs=[any_spec] * 5,
            out_specs=pl.BlockSpec(memory_space=pltpu.VMEM),
            scratch_shapes=[
                pltpu.VMEM(flow.shape, F32),
                pltpu.VMEM(point_pos.shape, F32),
                pltpu.VMEM(area_vec.shape, F32),
                pltpu.VMEM(observer_angles.shape, F32),
                pltpu.SMEM(band_offset.shape, jnp.int32),
                pltpu.VMEM((groups, 8, width), F32),
                pltpu.VMEM((2, 8, points), F32),
                pltpu.VMEM((2, 8, points), F32),
                pltpu.VMEM((4, steps, points), F32),
                pltpu.VMEM((4 * steps, 2 * points), BF16),
                pltpu.VMEM((steps, points), BF16),
                pltpu.VMEM((2, points, LAGS * width), BF16),
                pltpu.VMEM((2, 2 * points, LAGS * width), BF16),
                pltpu.VMEM((groups, steps + TAIL, width), F32),
                pltpu.VMEM((2, groups, 3 * steps, width), F32),
                dma((5,)),
                dma((groups,)),
                dma((groups,)),
                dma((2,)),
                dma((2,)),
                dma((2, groups)),
                dma((2, groups)),
            ],
            compiler_params=pltpu.CompilerParams(
                collective_id=0, has_side_effects=True, vmem_limit_bytes=40 * 1024 * 1024
            ),
        )(flow, point_pos, area_vec, observer_angles, band_offset)

    in_specs = (P(None, "tm", "obs"), P(None, "obs"), P(None, "obs"), P(None, "obs"), P())
    return jax.shard_map(
        local, mesh=mesh, in_specs=in_specs, out_specs=P("tm", "obs"), check_vma=False
    )
```

```python
import functools
import math

import jax
import jax.numpy as jnp
from jax import lax
from jax.experimental import pallas as pl
from jax.experimental.pallas import tpu as pltpu
from jax.sharding import PartitionSpec as P

LAGS = 4
FOUR_PI = 4.0 * math.pi
NEAR_RANGE = 3.25
SOUND_STEP = 1.17
SPHERE_RADIUS = 5.0
MESH = pl.DeviceIdType.MESH
F32 = jnp.float32
BF16 = jnp.bfloat16
TAIL = 8
CHUNK = 64


def split3(x):
    high = x.astype(BF16).astype(F32)
    rest = x - high
    mid = rest.astype(BF16).astype(F32)
    low = (rest - mid).astype(BF16).astype(F32)
    return high, mid, low


def squares(x):
    return x[0:1] * x[0:1] + x[1:2] * x[1:2] + x[2:3] * x[2:3]


def point_factors(points):
    scaled = FOUR_PI * points
    high, mid, low = split3(scaled)
    s_high, s_mid, s_low = split3(squares(scaled))
    ones = jnp.ones((3, points.shape[1]), F32)
    pad = jnp.zeros((8, points.shape[1]), F32)
    rows = [high, high, mid, high, low, mid, s_high, s_mid, s_low, ones, pad]
    return jnp.concatenate(rows, axis=0)


def observer_factors(places):
    scaled = FOUR_PI * places
    high, mid, low = split3(-2.0 * scaled)
    s_high, s_mid, s_low = split3(squares(scaled))
    ones = jnp.ones((3, places.shape[1]), F32)
    pad = jnp.zeros((8, places.shape[1]), F32)
    rows = [high, mid, high, low, high, mid, ones, s_high, s_mid, s_low, pad]
    return jnp.concatenate(rows, axis=0)


def fluxes(flow, area):
    density = 1.0 + 0.2 * flow[0]
    velocity = [0.4 * flow[1 + i] for i in range(3)]
    normal = velocity[0] * area[0:1] + velocity[1] * area[1:2] + velocity[2] * area[2:3]
    mass = density * normal
    return [mass] + [flow[4] * area[i : i + 1] + density * velocity[i] * normal for i in range(3)]


def kernel(
    groups, blocks,
    flow_hbm, pos_hbm, area_hbm, angles_hbm, band_hbm, out_ref,
    flow, pos, area, angles, band, places, edge_out, edge_in, flux, steady_rate, mass_rate,
    w_mass, w_load, sent, landed,
    in_sem, place_send, place_recv, edge_send, edge_recv, part_send, part_recv,
):
    me = lax.axis_index("obs")
    now = lax.axis_index("tm")
    steps = flow.shape[1]
    points = flow.shape[2]
    side = math.isqrt(groups)
    if side * side != groups:
        side = groups
    high, low = me // side, lax.rem(me, side)
    shifts = [(i, j) for i in range(groups // side) for j in range(side)]
    shifts.sort(key=lambda pair: (pair != (0, 0), -min(pair), -sum(pair)))
    order = [
        lax.rem(high + i, groups // side) * side + lax.rem(low + j, side) for i, j in shifts
    ]
    has_before = now > 0
    has_after = now < blocks - 1

    barrier = pltpu.get_barrier_semaphore()

    def greet(group, block):
        pl.semaphore_signal(barrier, inc=1, device_id=(group, block), device_id_type=MESH)

    for i in range(1, groups):
        greet(order[i], now)

    @pl.when(has_before)
    def _():
        for i in range(groups):
            greet(order[i], now - 1)

    @pl.when(has_after)
    def _():
        for i in range(groups):
            greet(order[i], now + 1)

    loads = [
        pltpu.make_async_copy(source, target, in_sem.at[i])
        for i, (source, target) in enumerate(
            [(angles_hbm, angles), (flow_hbm, flow), (area_hbm, area), (pos_hbm, pos), (band_hbm, band)]
        )
    ]
    for load in loads:
        load.start()

    loads[0].wait()
    azimuth = angles[0:1, :]
    elevation = angles[1:2, :]
    cos_e = jnp.cos(elevation)
    width = azimuth.shape[1]
    places[me] = jnp.concatenate(
        [
            SPHERE_RADIUS * (jnp.cos(azimuth) * cos_e),
            SPHERE_RADIUS * (jnp.sin(azimuth) * cos_e),
            SPHERE_RADIUS * jnp.sin(elevation),
            jnp.zeros((5, width), F32),
        ],
        axis=0,
    )

    loads[1].wait()
    loads[2].wait()
    area_rows = area[...]
    whole = fluxes(flow, area_rows)
    for k in range(4):
        flux[k] = whole[k]
    edge_pad = jnp.zeros((4, points), F32)
    edge_out[0] = jnp.concatenate([flux[k, 0:1, :] for k in range(4)] + [edge_pad], axis=0)
    edge_out[1] = jnp.concatenate(
        [flux[k, steps - 1 : steps, :] for k in range(4)] + [edge_pad], axis=0
    )

    neighbours = jnp.minimum(now, 1) + jnp.minimum(blocks - 1 - now, 1)
    pl.semaphore_wait(barrier, groups - 1 + groups * neighbours)

    def place_copy(i):
        return pltpu.make_async_remote_copy(
            src_ref=places.at[me], dst_ref=places.at[me],
            send_sem=place_send.at[i], recv_sem=place_recv.at[me],
            device_id=(order[i], now), device_id_type=MESH,
        )

    def edge_copy(side, block):
        return pltpu.make_async_remote_copy(
            src_ref=edge_out.at[side], dst_ref=edge_in.at[side],
            send_sem=edge_send.at[side], recv_sem=edge_recv.at[side],
            device_id=(me, block), device_id_type=MESH,
        )

    for i in range(1, groups):
        place_copy(i).start()

    @pl.when(has_before)
    def _():
        edge_copy(0, now - 1).start()

    @pl.when(has_after)
    def _():
        edge_copy(1, now + 1).start()

    for j in range(2):
        for b in range(groups):
            landed[j, b, 0:steps, :] = jnp.zeros((steps, width), F32)
            landed[j, b, 2 * steps + TAIL :, :] = jnp.zeros((steps - TAIL, width), F32)

    loads[3].wait()
    loads[4].wait()
    spots = pos[...]
    factors = jnp.transpose(point_factors(spots)).astype(BF16)
    spot_rows = [spots[i : i + 1, :] for i in range(3)]

    def with_projection(parts):
        rounded = [part.astype(BF16) for part in parts]
        wide = [part.astype(F32) for part in rounded]
        along = wide[0] * spot_rows[0] + wide[1] * spot_rows[1] + wide[2] * spot_rows[2]
        return jnp.concatenate(rounded + [(-along).astype(BF16)], axis=0)

    steady_rate[:, points:] = with_projection([flux[1 + k] for k in range(3)])

    near = 1.0 / (SOUND_STEP * FOUR_PI)
    slope = NEAR_RANGE / SOUND_STEP

    def weigh(slot, group_places):
        squared = jnp.dot(
            factors, observer_factors(group_places).astype(BF16), preferred_element_type=F32
        )
        for start in range(0, points, CHUNK):
            rows = slice(start, start + CHUNK)
            load_rows = slice(points + start, points + start + CHUNK)
            r = lax.rsqrt(squared[rows])
            u = near - slope * r
            z = u - r
            y = z - r
            tents = [
                jnp.maximum(0.0, -z),
                jnp.maximum(0.0, jnp.minimum(u, -y)),
                jnp.maximum(0.0, jnp.minimum(z, r - y)),
                jnp.maximum(0.0, y),
            ]
            by_rate = r * (FOUR_PI / SOUND_STEP)
            by_load = r * r * (FOUR_PI * FOUR_PI)
            for j in range(LAGS):
                columns = slice(j * width, (j + 1) * width)
                w_mass[slot, rows, columns] = tents[j].astype(BF16)
                w_load[slot, rows, columns] = (tents[j] * by_rate).astype(BF16)
                w_load[slot, load_rows, columns] = (tents[j] * by_load).astype(BF16)

    def part_copy(i, group, later):
        return pltpu.make_async_remote_copy(
            src_ref=sent.at[group], dst_ref=landed.at[later, me, pl.ds(steps, steps + TAIL), :],
            send_sem=part_send.at[later, i], recv_sem=part_recv.at[later, me],
            device_id=(group, now + later), device_id_type=MESH,
        )

    def await_places(i):
        pltpu.make_async_remote_copy(
            src_ref=places.at[order[i]], dst_ref=places.at[order[i]],
            send_sem=place_send.at[i], recv_sem=place_recv.at[order[i]],
            device_id=(order[i], now), device_id_type=MESH,
        ).wait_recv()

    weigh(0, places[me][0:3])

    @pl.when(has_before)
    def _():
        edge_copy(1, now - 1).wait_recv()

    @pl.when(has_after)
    def _():
        edge_copy(0, now + 1).wait_recv()

    @pl.when(jnp.logical_not(has_before))
    def _():
        edge_in[1] = jnp.zeros((8, points), F32)

    @pl.when(jnp.logical_not(has_after))
    def _():
        edge_in[0] = jnp.zeros((8, points), F32)

    row = lax.broadcasted_iota(jnp.int32, (steps, points), 0)
    rates = []
    for k in range(4):
        mine = flux[k]
        later = jnp.where(row == steps - 1, edge_in[0, k : k + 1, :], pltpu.roll(mine, steps - 1, 0))
        earlier = jnp.where(row == 0, edge_in[1, k : k + 1, :], pltpu.roll(mine, 1, 0))
        rates.append(0.5 * (later - earlier))
    mass_rate[...] = rates[0].astype(BF16)
    steady_rate[:, :points] = with_projection(rates[1:])

    for i in range(groups):
        group = order[i]
        slot = i % 2
        if i + 1 < groups:
            await_places(i + 1)
            weigh(1 - slot, places[order[i + 1]][0:3])
        group_places = places[group][0:3]
        by_mass = jnp.dot(mass_rate[...], w_mass[slot], preferred_element_type=F32)
        by_load = jnp.dot(steady_rate[...], w_load[slot], preferred_element_type=F32)
        total = jnp.zeros((steps + TAIL, width), F32)
        for j in range(LAGS):
            columns = slice(j * width, (j + 1) * width)
            piece = by_mass[:, columns] + by_load[3 * steps :, columns]
            for k in range(3):
                piece = piece + by_load[k * steps : (k + 1) * steps, columns] * group_places[k : k + 1]
            piece = jnp.concatenate([piece, jnp.zeros((TAIL, width), F32)], axis=0)
            total = total + (pltpu.roll(piece, j, 0) if j else piece)
        sent[group] = total
        if i > 0:
            part_copy(i, group, 0).start()
        else:
            landed[0, me, steps : 2 * steps + TAIL, :] = total

        @pl.when(has_after)
        def _():
            part_copy(i, group, 1).start()

    def arrived(later, block):
        return pltpu.make_async_remote_copy(
            src_ref=sent.at[0], dst_ref=landed.at[later, block, pl.ds(steps, steps + TAIL), :],
            send_sem=part_send.at[later, 0], recv_sem=part_recv.at[later, block],
            device_id=(order[1], now), device_id_type=MESH,
        )

    for i in range(1, groups):
        arrived(0, order[i]).wait_recv()

    @pl.when(has_before)
    def _():
        for b in range(groups):
            arrived(1, b).wait_recv()

    @pl.when(jnp.logical_not(has_before))
    def _():
        for b in range(groups):
            landed[1, b, steps : 2 * steps + TAIL, :] = jnp.zeros((steps + TAIL, width), F32)

    result = jnp.zeros((steps, width), F32)
    for b in range(groups):
        offset = band[me, b]
        result = result + landed[0, b, pl.ds(steps - offset, steps), :]
        result = result + landed[1, b, pl.ds(2 * steps - offset, steps), :]
    out_ref[...] = result

    for i in range(1, groups):
        place_copy(i).wait_send()
        part_copy(i, order[i], 0).wait_send()

    @pl.when(has_before)
    def _():
        edge_copy(0, now - 1).wait_send()

    @pl.when(has_after)
    def _():
        edge_copy(1, now + 1).wait_send()
        for i in range(groups):
            part_copy(i, order[i], 1).wait_send()


def solution(mesh):
    groups = mesh.shape["obs"]
    blocks = mesh.shape["tm"]

    def local(flow, point_pos, area_vec, observer_angles, band_offset):
        steps, points = flow.shape[1:]
        width = observer_angles.shape[1]
        any_spec = pl.BlockSpec(memory_space=pl.ANY)
        dma = pltpu.SemaphoreType.DMA
        return pl.pallas_call(
            functools.partial(kernel, groups, blocks),
            out_shape=jax.ShapeDtypeStruct((steps, width), F32),
            in_specs=[any_spec] * 5,
            out_specs=pl.BlockSpec(memory_space=pltpu.VMEM),
            scratch_shapes=[
                pltpu.VMEM(flow.shape, F32),
                pltpu.VMEM(point_pos.shape, F32),
                pltpu.VMEM(area_vec.shape, F32),
                pltpu.VMEM(observer_angles.shape, F32),
                pltpu.SMEM(band_offset.shape, jnp.int32),
                pltpu.VMEM((groups, 8, width), F32),
                pltpu.VMEM((2, 8, points), F32),
                pltpu.VMEM((2, 8, points), F32),
                pltpu.VMEM((4, steps, points), F32),
                pltpu.VMEM((4 * steps, 2 * points), BF16),
                pltpu.VMEM((steps, points), BF16),
                pltpu.VMEM((2, points, LAGS * width), BF16),
                pltpu.VMEM((2, 2 * points, LAGS * width), BF16),
                pltpu.VMEM((groups, steps + TAIL, width), F32),
                pltpu.VMEM((2, groups, 3 * steps, width), F32),
                dma((5,)),
                dma((groups,)),
                dma((groups,)),
                dma((2,)),
                dma((2,)),
                dma((2, groups)),
                dma((2, groups)),
            ],
            compiler_params=pltpu.CompilerParams(
                collective_id=0, has_side_effects=True, vmem_limit_bytes=64 * 1024 * 1024
            ),
        )(flow, point_pos, area_vec, observer_angles, band_offset)

    in_specs = (P(None, "tm", "obs"), P(None, "obs"), P(None, "obs"), P(None, "obs"), P())
    return jax.shard_map(
        local, mesh=mesh, in_specs=in_specs, out_specs=P("tm", "obs"), check_vma=False
    )
```

```python
import functools
import math

import jax
import jax.numpy as jnp
from jax import lax
from jax.experimental import pallas as pl
from jax.experimental.pallas import tpu as pltpu
from jax.sharding import PartitionSpec as P

LAGS = 4
FOUR_PI = 4.0 * math.pi
NEAR_RANGE = 3.25
SOUND_STEP = 1.17
SPHERE_RADIUS = 5.0
MESH = pl.DeviceIdType.MESH
F32 = jnp.float32
BF16 = jnp.bfloat16
TAIL = 8
CHUNK = 64


def split3(x):
    high = x.astype(BF16).astype(F32)
    rest = x - high
    mid = rest.astype(BF16).astype(F32)
    low = (rest - mid).astype(BF16).astype(F32)
    return high, mid, low


def squares(x):
    return x[0:1] * x[0:1] + x[1:2] * x[1:2] + x[2:3] * x[2:3]


def point_factors(points):
    scaled = FOUR_PI * points
    high, mid, low = split3(scaled)
    s_high, s_mid, s_low = split3(squares(scaled))
    ones = jnp.ones((3, points.shape[1]), F32)
    pad = jnp.zeros((8, points.shape[1]), F32)
    rows = [high, high, mid, high, low, mid, s_high, s_mid, s_low, ones, pad]
    return jnp.concatenate(rows, axis=0)


def observer_factors(places):
    scaled = FOUR_PI * places
    high, mid, low = split3(-2.0 * scaled)
    s_high, s_mid, s_low = split3(squares(scaled))
    ones = jnp.ones((3, places.shape[1]), F32)
    pad = jnp.zeros((8, places.shape[1]), F32)
    rows = [high, mid, high, low, high, mid, ones, s_high, s_mid, s_low, pad]
    return jnp.concatenate(rows, axis=0)


def fluxes(flow, area):
    density = 1.0 + 0.2 * flow[0]
    velocity = [0.4 * flow[1 + i] for i in range(3)]
    normal = velocity[0] * area[0:1] + velocity[1] * area[1:2] + velocity[2] * area[2:3]
    mass = density * normal
    return [mass] + [flow[4] * area[i : i + 1] + density * velocity[i] * normal for i in range(3)]


def kernel(
    groups, blocks,
    flow_hbm, pos_hbm, area_hbm, angles_hbm, band_hbm, out_ref,
    flow, pos, area, angles, band, places, edge_out, edge_in, flux, steady_rate, mass_rate,
    w_mass, w_load, sent, landed,
    in_sem, place_send, place_recv, edge_send, edge_recv, part_send, part_recv,
):
    me = lax.axis_index("obs")
    now = lax.axis_index("tm")
    steps = flow.shape[1]
    points = flow.shape[2]
    side = math.isqrt(groups)
    if side * side != groups:
        side = groups
    high, low = me // side, lax.rem(me, side)
    shifts = [(i, j) for i in range(groups // side) for j in range(side)]
    shifts.sort(key=lambda pair: (pair != (0, 0), -min(pair), -sum(pair)))
    order = [
        lax.rem(high + i, groups // side) * side + lax.rem(low + j, side) for i, j in shifts
    ]
    has_before = now > 0
    has_after = now < blocks - 1

    barrier = pltpu.get_barrier_semaphore()

    def greet(group, block):
        pl.semaphore_signal(barrier, inc=1, device_id=(group, block), device_id_type=MESH)

    for i in range(1, groups):
        greet(order[i], now)

    @pl.when(has_before)
    def _():
        for i in range(groups):
            greet(order[i], now - 1)

    @pl.when(has_after)
    def _():
        for i in range(groups):
            greet(order[i], now + 1)

    loads = [
        pltpu.make_async_copy(source, target, in_sem.at[i])
        for i, (source, target) in enumerate(
            [(angles_hbm, angles), (flow_hbm, flow), (area_hbm, area), (pos_hbm, pos), (band_hbm, band)]
        )
    ]
    for load in loads:
        load.start()

    loads[0].wait()
    azimuth = angles[0:1, :]
    elevation = angles[1:2, :]
    cos_e = jnp.cos(elevation)
    width = azimuth.shape[1]
    places[me] = jnp.concatenate(
        [
            SPHERE_RADIUS * (jnp.cos(azimuth) * cos_e),
            SPHERE_RADIUS * (jnp.sin(azimuth) * cos_e),
            SPHERE_RADIUS * jnp.sin(elevation),
            jnp.zeros((5, width), F32),
        ],
        axis=0,
    )

    loads[1].wait()
    loads[2].wait()
    area_rows = area[...]
    whole = fluxes(flow, area_rows)
    for k in range(4):
        flux[k] = whole[k]
    edge_pad = jnp.zeros((4, points), F32)
    edge_out[0] = jnp.concatenate([flux[k, 0:1, :] for k in range(4)] + [edge_pad], axis=0)
    edge_out[1] = jnp.concatenate(
        [flux[k, steps - 1 : steps, :] for k in range(4)] + [edge_pad], axis=0
    )

    neighbours = jnp.minimum(now, 1) + jnp.minimum(blocks - 1 - now, 1)
    pl.semaphore_wait(barrier, groups - 1 + groups * neighbours)

    def place_copy(i):
        return pltpu.make_async_remote_copy(
            src_ref=places.at[me], dst_ref=places.at[me],
            send_sem=place_send.at[i], recv_sem=place_recv.at[me],
            device_id=(order[i], now), device_id_type=MESH,
        )

    def edge_copy(side, block):
        return pltpu.make_async_remote_copy(
            src_ref=edge_out.at[side], dst_ref=edge_in.at[side],
            send_sem=edge_send.at[side], recv_sem=edge_recv.at[side],
            device_id=(me, block), device_id_type=MESH,
        )

    for i in range(1, groups):
        place_copy(i).start()

    @pl.when(has_before)
    def _():
        edge_copy(0, now - 1).start()

    @pl.when(has_after)
    def _():
        edge_copy(1, now + 1).start()

    for j in range(2):
        for b in range(groups):
            landed[j, b, 0:steps, :] = jnp.zeros((steps, width), F32)
            landed[j, b, 2 * steps + TAIL :, :] = jnp.zeros((steps - TAIL, width), F32)

    loads[3].wait()
    loads[4].wait()
    spots = pos[...]
    factors = jnp.transpose(point_factors(spots)).astype(BF16)
    spot_rows = [spots[i : i + 1, :] for i in range(3)]

    def with_projection(parts):
        rounded = [part.astype(BF16) for part in parts]
        wide = [part.astype(F32) for part in rounded]
        along = wide[0] * spot_rows[0] + wide[1] * spot_rows[1] + wide[2] * spot_rows[2]
        return jnp.concatenate(rounded + [(-along).astype(BF16)], axis=0)

    steady_rate[:, points:] = with_projection([flux[1 + k] for k in range(3)])

    near = 1.0 / (SOUND_STEP * FOUR_PI)
    slope = NEAR_RANGE / SOUND_STEP

    def weigh(slot, group_places):
        squared = jnp.dot(
            factors, observer_factors(group_places).astype(BF16), preferred_element_type=F32
        )
        for start in range(0, points, CHUNK):
            rows = slice(start, start + CHUNK)
            load_rows = slice(points + start, points + start + CHUNK)
            r = lax.rsqrt(squared[rows])
            u = near - slope * r
            z = u - r
            y = z - r
            tents = [
                jnp.maximum(0.0, -z),
                jnp.maximum(0.0, jnp.minimum(u, -y)),
                jnp.maximum(0.0, jnp.minimum(z, r - y)),
                jnp.maximum(0.0, y),
            ]
            by_rate = r * (FOUR_PI / SOUND_STEP)
            by_load = r * r * (FOUR_PI * FOUR_PI)
            for j in range(LAGS):
                columns = slice(j * width, (j + 1) * width)
                w_mass[slot, rows, columns] = tents[j].astype(BF16)
                w_load[slot, rows, columns] = (tents[j] * by_rate).astype(BF16)
                w_load[slot, load_rows, columns] = (tents[j] * by_load).astype(BF16)

    def part_copy(i, group, later):
        return pltpu.make_async_remote_copy(
            src_ref=sent.at[group], dst_ref=landed.at[later, me, pl.ds(steps, steps + TAIL), :],
            send_sem=part_send.at[later, i], recv_sem=part_recv.at[later, me],
            device_id=(group, now + later), device_id_type=MESH,
        )

    def await_places(i):
        pltpu.make_async_remote_copy(
            src_ref=places.at[order[i]], dst_ref=places.at[order[i]],
            send_sem=place_send.at[i], recv_sem=place_recv.at[order[i]],
            device_id=(order[i], now), device_id_type=MESH,
        ).wait_recv()

    weigh(0, places[me][0:3])

    @pl.when(has_before)
    def _():
        edge_copy(1, now - 1).wait_recv()

    @pl.when(has_after)
    def _():
        edge_copy(0, now + 1).wait_recv()

    @pl.when(jnp.logical_not(has_before))
    def _():
        edge_in[1] = jnp.zeros((8, points), F32)

    @pl.when(jnp.logical_not(has_after))
    def _():
        edge_in[0] = jnp.zeros((8, points), F32)

    row = lax.broadcasted_iota(jnp.int32, (steps, points), 0)
    rates = []
    for k in range(4):
        mine = flux[k]
        later = jnp.where(row == steps - 1, edge_in[0, k : k + 1, :], pltpu.roll(mine, steps - 1, 0))
        earlier = jnp.where(row == 0, edge_in[1, k : k + 1, :], pltpu.roll(mine, 1, 0))
        rates.append(0.5 * (later - earlier))
    mass_rate[...] = rates[0].astype(BF16)
    steady_rate[:, :points] = with_projection(rates[1:])

    for i in range(groups):
        group = order[i]
        slot = i % 2
        if i + 1 < groups:
            await_places(i + 1)
            weigh(1 - slot, places[order[i + 1]][0:3])
        group_places = places[group][0:3]
        by_mass = jnp.dot(mass_rate[...], w_mass[slot], preferred_element_type=F32)
        by_load = jnp.dot(steady_rate[...], w_load[slot], preferred_element_type=F32)
        total = jnp.zeros((steps + TAIL, width), F32)
        for j in range(LAGS):
            columns = slice(j * width, (j + 1) * width)
            piece = by_mass[:, columns] + by_load[3 * steps :, columns]
            for k in range(3):
                piece = piece + by_load[k * steps : (k + 1) * steps, columns] * group_places[k : k + 1]
            piece = jnp.concatenate([piece, jnp.zeros((TAIL, width), F32)], axis=0)
            total = total + (pltpu.roll(piece, j, 0) if j else piece)
        sent[group] = total
        if i > 0:
            part_copy(i, group, 0).start()
        else:
            landed[0, me, steps : 2 * steps + TAIL, :] = total

        @pl.when(has_after)
        def _():
            part_copy(i, group, 1).start()

    def arrived(later, block):
        return pltpu.make_async_remote_copy(
            src_ref=sent.at[0], dst_ref=landed.at[later, block, pl.ds(steps, steps + TAIL), :],
            send_sem=part_send.at[later, 0], recv_sem=part_recv.at[later, block],
            device_id=(order[1], now), device_id_type=MESH,
        )

    for i in range(1, groups):
        arrived(0, order[i]).wait_recv()

    @pl.when(has_before)
    def _():
        for b in range(groups):
            arrived(1, b).wait_recv()

    @pl.when(jnp.logical_not(has_before))
    def _():
        for b in range(groups):
            landed[1, b, steps : 2 * steps + TAIL, :] = jnp.zeros((steps + TAIL, width), F32)

    result = jnp.zeros((steps, width), F32)
    for b in range(groups):
        offset = band[me, b]
        result = result + landed[0, b, pl.ds(steps - offset, steps), :]
        result = result + landed[1, b, pl.ds(2 * steps - offset, steps), :]
    out_ref[...] = result

    for i in range(1, groups):
        place_copy(i).wait_send()
        part_copy(i, order[i], 0).wait_send()

    @pl.when(has_before)
    def _():
        edge_copy(0, now - 1).wait_send()

    @pl.when(has_after)
    def _():
        edge_copy(1, now + 1).wait_send()
        for i in range(groups):
            part_copy(i, order[i], 1).wait_send()


def solution(mesh):
    groups = mesh.shape["obs"]
    blocks = mesh.shape["tm"]

    def local(flow, point_pos, area_vec, observer_angles, band_offset):
        steps, points = flow.shape[1:]
        width = observer_angles.shape[1]
        any_spec = pl.BlockSpec(memory_space=pl.ANY)
        dma = pltpu.SemaphoreType.DMA
        return pl.pallas_call(
            functools.partial(kernel, groups, blocks),
            out_shape=jax.ShapeDtypeStruct((steps, width), F32),
            in_specs=[any_spec] * 5,
            out_specs=pl.BlockSpec(memory_space=pltpu.VMEM),
            scratch_shapes=[
                pltpu.VMEM(flow.shape, F32),
                pltpu.VMEM(point_pos.shape, F32),
                pltpu.VMEM(area_vec.shape, F32),
                pltpu.VMEM(observer_angles.shape, F32),
                pltpu.SMEM(band_offset.shape, jnp.int32),
                pltpu.VMEM((groups, 8, width), F32),
                pltpu.VMEM((2, 8, points), F32),
                pltpu.VMEM((2, 8, points), F32),
                pltpu.VMEM((4, steps, points), F32),
                pltpu.VMEM((4 * steps, 2 * points), BF16),
                pltpu.VMEM((steps, points), BF16),
                pltpu.VMEM((2, points, LAGS * width), BF16),
                pltpu.VMEM((2, 2 * points, LAGS * width), BF16),
                pltpu.VMEM((groups, steps + TAIL, width), F32),
                pltpu.VMEM((2, groups, 3 * steps, width), F32),
                dma((5,)),
                dma((groups,)),
                dma((groups,)),
                dma((2,)),
                dma((2,)),
                dma((2, groups)),
                dma((2, groups)),
            ],
            compiler_params=pltpu.CompilerParams(
                collective_id=0, has_side_effects=True, vmem_limit_bytes=40 * 1024 * 1024
            ),
        )(
            *[
                pltpu.with_memory_space_constraint(x, pltpu.HBM)
                for x in (flow, point_pos, area_vec, observer_angles, band_offset)
            ]
        )

    in_specs = (P(None, "tm", "obs"), P(None, "obs"), P(None, "obs"), P(None, "obs"), P())
    return jax.shard_map(
        local, mesh=mesh, in_specs=in_specs, out_specs=P("tm", "obs"), check_vma=False
    )
```

```python
import functools
import math

import jax
import jax.numpy as jnp
from jax import lax
from jax.experimental import pallas as pl
from jax.experimental.pallas import tpu as pltpu
from jax.sharding import PartitionSpec as P

LAGS = 4
FOUR_PI = 4.0 * math.pi
NEAR_RANGE = 3.25
SOUND_STEP = 1.17
SPHERE_RADIUS = 5.0
MESH = pl.DeviceIdType.MESH
F32 = jnp.float32
BF16 = jnp.bfloat16
TAIL = 8
CHUNK = 64


def split3(x):
    high = x.astype(BF16).astype(F32)
    rest = x - high
    mid = rest.astype(BF16).astype(F32)
    low = (rest - mid).astype(BF16).astype(F32)
    return high, mid, low


def squares(x):
    return x[0:1] * x[0:1] + x[1:2] * x[1:2] + x[2:3] * x[2:3]


def point_factors(points):
    scaled = FOUR_PI * points
    high, mid, low = split3(scaled)
    s_high, s_mid, s_low = split3(squares(scaled))
    ones = jnp.ones((3, points.shape[1]), F32)
    pad = jnp.zeros((8, points.shape[1]), F32)
    rows = [high, high, mid, high, low, mid, s_high, s_mid, s_low, ones, pad]
    return jnp.concatenate(rows, axis=0)


def observer_factors(places):
    scaled = FOUR_PI * places
    high, mid, low = split3(-2.0 * scaled)
    s_high, s_mid, s_low = split3(squares(scaled))
    ones = jnp.ones((3, places.shape[1]), F32)
    pad = jnp.zeros((8, places.shape[1]), F32)
    rows = [high, mid, high, low, high, mid, ones, s_high, s_mid, s_low, pad]
    return jnp.concatenate(rows, axis=0)


def fluxes(flow, area):
    density = 1.0 + 0.2 * flow[0]
    velocity = [0.4 * flow[1 + i] for i in range(3)]
    normal = velocity[0] * area[0:1] + velocity[1] * area[1:2] + velocity[2] * area[2:3]
    mass = density * normal
    return [mass] + [flow[4] * area[i : i + 1] + density * velocity[i] * normal for i in range(3)]


def kernel(
    groups, blocks,
    flow_hbm, pos_hbm, area_hbm, angles_hbm, band_hbm, out_ref,
    flow, pos, area, angles, band, places, edge_out, edge_in, flux, steady_rate, mass_rate,
    w_mass_low, w_mass_high, w_load_low, w_load_high, factors, inverse, sent, landed,
    in_sem, place_send, place_recv, edge_send, edge_recv, part_send, part_recv,
):
    w_mass = (w_mass_low, w_mass_high)
    w_load = (w_load_low, w_load_high)
    me = lax.axis_index("obs")
    now = lax.axis_index("tm")
    steps = flow.shape[1]
    points = flow.shape[2]
    side = math.isqrt(groups)
    if side * side != groups:
        side = groups
    high, low = me // side, lax.rem(me, side)

    def order(i):
        shift = lax.rem(groups - i, groups)
        row_index = lax.rem(high + shift // side, groups // side)
        return row_index * side + lax.rem(low + lax.rem(shift, side), side)

    has_before = now > 0
    has_after = now < blocks - 1

    barrier = pltpu.get_barrier_semaphore()

    def greet(group, block):
        pl.semaphore_signal(barrier, inc=1, device_id=(group, block), device_id_type=MESH)

    for i in range(1, groups):
        greet(order(i), now)

    @pl.when(has_before)
    def _():
        for i in range(groups):
            greet(order(i), now - 1)

    @pl.when(has_after)
    def _():
        for i in range(groups):
            greet(order(i), now + 1)

    loads = [
        pltpu.make_async_copy(source, target, in_sem.at[i])
        for i, (source, target) in enumerate(
            [(angles_hbm, angles), (flow_hbm, flow), (area_hbm, area), (pos_hbm, pos), (band_hbm, band)]
        )
    ]
    for load in loads:
        load.start()

    loads[0].wait()
    azimuth = angles[0:1, :]
    elevation = angles[1:2, :]
    cos_e = jnp.cos(elevation)
    width = azimuth.shape[1]
    places[me] = jnp.concatenate(
        [
            SPHERE_RADIUS * (jnp.cos(azimuth) * cos_e),
            SPHERE_RADIUS * (jnp.sin(azimuth) * cos_e),
            SPHERE_RADIUS * jnp.sin(elevation),
            jnp.zeros((5, width), F32),
        ],
        axis=0,
    )

    loads[1].wait()
    loads[2].wait()
    area_rows = area[...]
    whole = fluxes(flow, area_rows)
    for k in range(4):
        flux[k] = whole[k]
    edge_pad = jnp.zeros((4, points), F32)
    edge_out[0] = jnp.concatenate([flux[k, 0:1, :] for k in range(4)] + [edge_pad], axis=0)
    edge_out[1] = jnp.concatenate(
        [flux[k, steps - 1 : steps, :] for k in range(4)] + [edge_pad], axis=0
    )

    neighbours = jnp.minimum(now, 1) + jnp.minimum(blocks - 1 - now, 1)
    pl.semaphore_wait(barrier, groups - 1 + groups * neighbours)

    def place_copy(i):
        return pltpu.make_async_remote_copy(
            src_ref=places.at[me], dst_ref=places.at[me],
            send_sem=place_send.at[i], recv_sem=place_recv.at[me],
            device_id=(order(i), now), device_id_type=MESH,
        )

    def edge_copy(side, block):
        return pltpu.make_async_remote_copy(
            src_ref=edge_out.at[side], dst_ref=edge_in.at[side],
            send_sem=edge_send.at[side], recv_sem=edge_recv.at[side],
            device_id=(me, block), device_id_type=MESH,
        )

    for i in range(1, groups):
        place_copy(i).start()

    @pl.when(has_before)
    def _():
        edge_copy(0, now - 1).start()

    @pl.when(has_after)
    def _():
        edge_copy(1, now + 1).start()

    for j in range(2):
        for b in range(groups):
            landed[j, b, 0:steps, :] = jnp.zeros((steps, width), F32)
            landed[j, b, 2 * steps + TAIL :, :] = jnp.zeros((steps - TAIL, width), F32)

    loads[3].wait()
    loads[4].wait()
    spots = pos[...]
    factors[...] = jnp.transpose(point_factors(spots)).astype(BF16)
    spot_rows = [spots[i : i + 1, :] for i in range(3)]

    def with_projection(parts):
        rounded = [part.astype(BF16) for part in parts]
        wide = [part.astype(F32) for part in rounded]
        along = wide[0] * spot_rows[0] + wide[1] * spot_rows[1] + wide[2] * spot_rows[2]
        return jnp.concatenate(rounded + [(-along).astype(BF16)], axis=0)

    steady_rate[:, points:] = with_projection([flux[1 + k] for k in range(3)])

    near = 1.0 / (SOUND_STEP * FOUR_PI)
    slope = NEAR_RANGE / SOUND_STEP

    def weigh(pair, squared):
        for start in range(0, points, CHUNK):
            rows = slice(start, start + CHUNK)
            load_rows = slice(points + start, points + start + CHUNK)
            if pair == 0:
                r = lax.rsqrt(squared[rows])
                inverse[rows, :] = r
            else:
                r = inverse[rows, :]
            u = near - slope * r
            z = u - r
            y = z - r
            if pair == 0:
                tents = [jnp.maximum(0.0, -z), jnp.maximum(0.0, jnp.minimum(u, -y))]
            else:
                tents = [jnp.maximum(0.0, jnp.minimum(z, r - y)), jnp.maximum(0.0, y)]
            by_rate = r * (FOUR_PI / SOUND_STEP)
            by_load = r * r * (FOUR_PI * FOUR_PI)
            for j in range(2):
                columns = slice(j * width, (j + 1) * width)
                w_mass[pair][rows, columns] = tents[j].astype(BF16)
                w_load[pair][rows, columns] = (tents[j] * by_rate).astype(BF16)
                w_load[pair][load_rows, columns] = (tents[j] * by_load).astype(BF16)

    def ranges(group):
        return jnp.dot(
            factors[...],
            observer_factors(places[group][0:3]).astype(BF16),
            preferred_element_type=F32,
        )

    def part_copy(i, group, later):
        return pltpu.make_async_remote_copy(
            src_ref=sent.at[group], dst_ref=landed.at[later, me, pl.ds(steps, steps + TAIL), :],
            send_sem=part_send.at[later, i], recv_sem=part_recv.at[later, me],
            device_id=(group, now + later), device_id_type=MESH,
        )

    def await_places(i):
        pltpu.make_async_remote_copy(
            src_ref=places.at[order(i)], dst_ref=places.at[order(i)],
            send_sem=place_send.at[i], recv_sem=place_recv.at[order(i)],
            device_id=(order(i), now), device_id_type=MESH,
        ).wait_recv()

    weigh(0, ranges(me))

    @pl.when(has_before)
    def _():
        edge_copy(1, now - 1).wait_recv()

    @pl.when(has_after)
    def _():
        edge_copy(0, now + 1).wait_recv()

    @pl.when(jnp.logical_not(has_before))
    def _():
        edge_in[1] = jnp.zeros((8, points), F32)

    @pl.when(jnp.logical_not(has_after))
    def _():
        edge_in[0] = jnp.zeros((8, points), F32)

    row = lax.broadcasted_iota(jnp.int32, (steps, points), 0)
    rates = []
    for k in range(4):
        mine = flux[k]
        later = jnp.where(row == steps - 1, edge_in[0, k : k + 1, :], pltpu.roll(mine, steps - 1, 0))
        earlier = jnp.where(row == 0, edge_in[1, k : k + 1, :], pltpu.roll(mine, 1, 0))
        rates.append(0.5 * (later - earlier))
    mass_rate[...] = rates[0].astype(BF16)
    steady_rate[:, :points] = with_projection(rates[1:])

    def gathered(pair, group):
        spot = places[group]
        by_mass = jnp.dot(mass_rate[...], w_mass[pair][...], preferred_element_type=F32)
        by_load = jnp.dot(steady_rate[...], w_load[pair][...], preferred_element_type=F32)
        total = jnp.zeros((steps + TAIL, width), F32)
        for j in range(2):
            columns = slice(j * width, (j + 1) * width)
            piece = by_mass[:, columns] + by_load[3 * steps :, columns]
            for k in range(3):
                piece = piece + by_load[k * steps : (k + 1) * steps, columns] * spot[k : k + 1]
            piece = jnp.concatenate([piece, jnp.zeros((TAIL, width), F32)], axis=0)
            lag = 2 * pair + j
            total = total + (pltpu.roll(piece, lag, 0) if lag else piece)
        return total

    def one_group(i, unused):
        group = order(i)
        sent[group] = gathered(0, group)
        weigh(1, None)

        @pl.when(i + 1 < groups)
        def _():
            await_places(i + 1)

        total = sent[group] + gathered(1, group)
        sent[group] = total
        weigh(0, ranges(order(jnp.minimum(i + 1, groups - 1))))

        @pl.when(i > 0)
        def _():
            part_copy(i, group, 0).start()

        @pl.when(i == 0)
        def _():
            landed[0, me, steps : 2 * steps + TAIL, :] = sent[me]

        @pl.when(has_after)
        def _():
            part_copy(i, group, 1).start()

        return unused

    lax.fori_loop(0, groups, one_group, 0)

    def arrived(later, block):
        return pltpu.make_async_remote_copy(
            src_ref=sent.at[0], dst_ref=landed.at[later, block, pl.ds(steps, steps + TAIL), :],
            send_sem=part_send.at[later, 0], recv_sem=part_recv.at[later, block],
            device_id=(order(1), now), device_id_type=MESH,
        )

    for i in range(1, groups):
        arrived(0, order(i)).wait_recv()

    @pl.when(has_before)
    def _():
        for b in range(groups):
            arrived(1, b).wait_recv()

    @pl.when(jnp.logical_not(has_before))
    def _():
        for b in range(groups):
            landed[1, b, steps : 2 * steps + TAIL, :] = jnp.zeros((steps + TAIL, width), F32)

    result = jnp.zeros((steps, width), F32)
    for b in range(groups):
        offset = band[me, b]
        result = result + landed[0, b, pl.ds(steps - offset, steps), :]
        result = result + landed[1, b, pl.ds(2 * steps - offset, steps), :]
    out_ref[...] = result

    for i in range(1, groups):
        place_copy(i).wait_send()
        part_copy(i, order(i), 0).wait_send()

    @pl.when(has_before)
    def _():
        edge_copy(0, now - 1).wait_send()

    @pl.when(has_after)
    def _():
        edge_copy(1, now + 1).wait_send()
        for i in range(groups):
            part_copy(i, order(i), 1).wait_send()


def solution(mesh):
    groups = mesh.shape["obs"]
    blocks = mesh.shape["tm"]

    def local(flow, point_pos, area_vec, observer_angles, band_offset):
        steps, points = flow.shape[1:]
        width = observer_angles.shape[1]
        any_spec = pl.BlockSpec(memory_space=pl.ANY)
        dma = pltpu.SemaphoreType.DMA
        return pl.pallas_call(
            functools.partial(kernel, groups, blocks),
            out_shape=jax.ShapeDtypeStruct((steps, width), F32),
            in_specs=[any_spec] * 5,
            out_specs=pl.BlockSpec(memory_space=pltpu.VMEM),
            scratch_shapes=[
                pltpu.VMEM(flow.shape, F32),
                pltpu.VMEM(point_pos.shape, F32),
                pltpu.VMEM(area_vec.shape, F32),
                pltpu.VMEM(observer_angles.shape, F32),
                pltpu.SMEM(band_offset.shape, jnp.int32),
                pltpu.VMEM((groups, 8, width), F32),
                pltpu.VMEM((2, 8, points), F32),
                pltpu.VMEM((2, 8, points), F32),
                pltpu.VMEM((4, steps, points), F32),
                pltpu.VMEM((4 * steps, 2 * points), BF16),
                pltpu.VMEM((steps, points), BF16),
                pltpu.VMEM((points, LAGS // 2 * width), BF16),
                pltpu.VMEM((points, LAGS // 2 * width), BF16),
                pltpu.VMEM((2 * points, LAGS // 2 * width), BF16),
                pltpu.VMEM((2 * points, LAGS // 2 * width), BF16),
                pltpu.VMEM((points, 32), BF16),
                pltpu.VMEM((points, width), F32),
                pltpu.VMEM((groups, steps + TAIL, width), F32),
                pltpu.VMEM((2, groups, 3 * steps, width), F32),
                dma((5,)),
                dma((groups,)),
                dma((groups,)),
                dma((2,)),
                dma((2,)),
                dma((2, groups)),
                dma((2, groups)),
            ],
            compiler_params=pltpu.CompilerParams(
                collective_id=0, has_side_effects=True, vmem_limit_bytes=40 * 1024 * 1024
            ),
        )(
            *[
                pltpu.with_memory_space_constraint(x, pltpu.HBM)
                for x in (flow, point_pos, area_vec, observer_angles, band_offset)
            ]
        )

    in_specs = (P(None, "tm", "obs"), P(None, "obs"), P(None, "obs"), P(None, "obs"), P())
    return jax.shard_map(
        local, mesh=mesh, in_specs=in_specs, out_specs=P("tm", "obs"), check_vma=False
    )
```

```python
import functools
import math

import jax
import jax.numpy as jnp
from jax import lax
from jax.experimental import pallas as pl
from jax.experimental.pallas import tpu as pltpu
from jax.sharding import PartitionSpec as P

LAGS = 4
FOUR_PI = 4.0 * math.pi
NEAR_RANGE = 3.25
SOUND_STEP = 1.17
SPHERE_RADIUS = 5.0
MESH = pl.DeviceIdType.MESH
F32 = jnp.float32
BF16 = jnp.bfloat16
TAIL = 8
CHUNK = 64


def split3(x):
    high = x.astype(BF16).astype(F32)
    rest = x - high
    mid = rest.astype(BF16).astype(F32)
    low = (rest - mid).astype(BF16).astype(F32)
    return high, mid, low


def squares(x):
    return x[0:1] * x[0:1] + x[1:2] * x[1:2] + x[2:3] * x[2:3]


def point_factors(points):
    scaled = FOUR_PI * points
    high, mid, low = split3(scaled)
    s_high, s_mid, s_low = split3(squares(scaled))
    ones = jnp.ones((3, points.shape[1]), F32)
    pad = jnp.zeros((8, points.shape[1]), F32)
    rows = [high, high, mid, high, low, mid, s_high, s_mid, s_low, ones, pad]
    return jnp.concatenate(rows, axis=0)


def observer_factors(places):
    scaled = FOUR_PI * places
    high, mid, low = split3(-2.0 * scaled)
    s_high, s_mid, s_low = split3(squares(scaled))
    ones = jnp.ones((3, places.shape[1]), F32)
    pad = jnp.zeros((8, places.shape[1]), F32)
    rows = [high, mid, high, low, high, mid, ones, s_high, s_mid, s_low, pad]
    return jnp.concatenate(rows, axis=0)


def sine_cosine(x):
    turns = jnp.floor(x * (2.0 / math.pi) + 0.5)
    r = ((x - turns * 1.5703125) - turns * 4.8351287841796875e-4) - turns * 3.13855707645416259e-07
    r2 = r * r
    sine = r + r * r2 * (-1.6666654611e-1 + r2 * (8.3321608736e-3 + r2 * -1.9515295891e-4))
    cosine = (1.0 - 0.5 * r2) + r2 * r2 * (
        4.166664568298827e-2 + r2 * (-1.388731625493765e-3 + r2 * 2.443315711809948e-5)
    )
    quadrant = turns.astype(jnp.int32) & 3
    odd = (quadrant & 1) == 1
    first = jnp.where(odd, cosine, sine)
    second = jnp.where(odd, sine, cosine)
    sine = jnp.where(quadrant >= 2, -first, first)
    cosine = jnp.where((quadrant == 1) | (quadrant == 2), -second, second)
    return sine, cosine


def fluxes(flow, area):
    density = 1.0 + 0.2 * flow[0]
    velocity = [0.4 * flow[1 + i] for i in range(3)]
    normal = velocity[0] * area[0:1] + velocity[1] * area[1:2] + velocity[2] * area[2:3]
    mass = density * normal
    return [mass] + [flow[4] * area[i : i + 1] + density * velocity[i] * normal for i in range(3)]


def kernel(
    groups, blocks,
    flow_hbm, pos_hbm, area_hbm, angles_hbm, band_hbm, out_ref,
    flow, pos, area, angles, band, places, edge_out, edge_in, flux, steady_rate, mass_rate,
    w_mass, w_load, sent, landed,
    in_sem, place_send, place_recv, edge_send, edge_recv, part_send, part_recv,
):
    me = lax.axis_index("obs")
    now = lax.axis_index("tm")
    steps = flow.shape[1]
    points = flow.shape[2]
    side = math.isqrt(groups)
    if side * side != groups:
        side = groups
    high, low = me // side, lax.rem(me, side)
    shifts = [(i, j) for i in range(groups // side) for j in range(side)]
    shifts.sort(key=lambda pair: (pair != (0, 0), -min(pair), -sum(pair)))
    order = [
        lax.rem(high + i, groups // side) * side + lax.rem(low + j, side) for i, j in shifts
    ]
    has_before = now > 0
    has_after = now < blocks - 1

    barrier = pltpu.get_barrier_semaphore()

    def greet(group, block):
        pl.semaphore_signal(barrier, inc=1, device_id=(group, block), device_id_type=MESH)

    for i in range(1, groups):
        greet(order[i], now)

    @pl.when(has_before)
    def _():
        for i in range(groups):
            greet(order[i], now - 1)

    @pl.when(has_after)
    def _():
        for i in range(groups):
            greet(order[i], now + 1)

    loads = [
        pltpu.make_async_copy(source, target, in_sem.at[i])
        for i, (source, target) in enumerate(
            [(angles_hbm, angles), (flow_hbm, flow), (area_hbm, area), (pos_hbm, pos), (band_hbm, band)]
        )
    ]
    for load in loads:
        load.start()

    loads[0].wait()
    width = angles.shape[1]
    sine, cosine = sine_cosine(angles[...])
    cos_e = cosine[1:2]
    places[me] = jnp.concatenate(
        [
            SPHERE_RADIUS * (cosine[0:1] * cos_e),
            SPHERE_RADIUS * (sine[0:1] * cos_e),
            SPHERE_RADIUS * sine[1:2],
            jnp.zeros((5, width), F32),
        ],
        axis=0,
    )

    neighbours = jnp.minimum(now, 1) + jnp.minimum(blocks - 1 - now, 1)
    pl.semaphore_wait(barrier, groups - 1 + groups * neighbours)

    def place_copy(i):
        return pltpu.make_async_remote_copy(
            src_ref=places.at[me], dst_ref=places.at[me],
            send_sem=place_send.at[i], recv_sem=place_recv.at[me],
            device_id=(order[i], now), device_id_type=MESH,
        )

    for i in range(1, groups):
        place_copy(i).start()

    loads[1].wait()
    loads[2].wait()
    area_rows = area[...]
    whole = fluxes(flow, area_rows)
    for k in range(4):
        flux[k] = whole[k]
    edge_pad = jnp.zeros((4, points), F32)
    edge_out[0] = jnp.concatenate([flux[k, 0:1, :] for k in range(4)] + [edge_pad], axis=0)
    edge_out[1] = jnp.concatenate(
        [flux[k, steps - 1 : steps, :] for k in range(4)] + [edge_pad], axis=0
    )

    def edge_copy(side, block):
        return pltpu.make_async_remote_copy(
            src_ref=edge_out.at[side], dst_ref=edge_in.at[side],
            send_sem=edge_send.at[side], recv_sem=edge_recv.at[side],
            device_id=(me, block), device_id_type=MESH,
        )

    @pl.when(has_before)
    def _():
        edge_copy(0, now - 1).start()

    @pl.when(has_after)
    def _():
        edge_copy(1, now + 1).start()

    for j in range(2):
        for b in range(groups):
            landed[j, b, 0:steps, :] = jnp.zeros((steps, width), F32)
            landed[j, b, 2 * steps + TAIL :, :] = jnp.zeros((steps - TAIL, width), F32)

    @pl.when(jnp.logical_not(has_before))
    def _():
        for b in range(groups):
            landed[1, b, steps : 2 * steps + TAIL, :] = jnp.zeros((steps + TAIL, width), F32)

    loads[3].wait()
    loads[4].wait()
    spots = pos[...]
    factors = jnp.transpose(point_factors(spots)).astype(BF16)
    spot_rows = [spots[i : i + 1, :] for i in range(3)]

    def with_projection(parts):
        rounded = [part.astype(BF16) for part in parts]
        wide = [part.astype(F32) for part in rounded]
        along = wide[0] * spot_rows[0] + wide[1] * spot_rows[1] + wide[2] * spot_rows[2]
        return jnp.concatenate(rounded + [(-along).astype(BF16)], axis=0)

    steady_rate[:, points:] = with_projection([flux[1 + k] for k in range(3)])

    near = 1.0 / (SOUND_STEP * FOUR_PI)
    slope = NEAR_RANGE / SOUND_STEP

    def weigh(slot, group_places):
        squared = jnp.dot(
            factors, observer_factors(group_places).astype(BF16), preferred_element_type=F32
        )
        for start in range(0, points, CHUNK):
            rows = slice(start, start + CHUNK)
            load_rows = slice(points + start, points + start + CHUNK)
            r = lax.rsqrt(squared[rows])
            u = near - slope * r
            z = u - r
            y = z - r
            tents = [
                jnp.maximum(0.0, -z),
                jnp.maximum(0.0, jnp.minimum(u, -y)),
                jnp.maximum(0.0, jnp.minimum(z, r - y)),
                jnp.maximum(0.0, y),
            ]
            by_rate = r * (FOUR_PI / SOUND_STEP)
            by_load = r * r * (FOUR_PI * FOUR_PI)
            for j in range(LAGS):
                columns = slice(j * width, (j + 1) * width)
                w_mass[slot, rows, columns] = tents[j].astype(BF16)
                w_load[slot, rows, columns] = (tents[j] * by_rate).astype(BF16)
                w_load[slot, load_rows, columns] = (tents[j] * by_load).astype(BF16)

    def part_copy(i, group, later):
        count = steps + TAIL * later
        return pltpu.make_async_remote_copy(
            src_ref=sent.at[group, pl.ds(0, count), :],
            dst_ref=landed.at[later, me, pl.ds(steps, count), :],
            send_sem=part_send.at[later, i], recv_sem=part_recv.at[later, me],
            device_id=(group, now + later), device_id_type=MESH,
        )

    def await_places(i):
        pltpu.make_async_remote_copy(
            src_ref=places.at[order[i]], dst_ref=places.at[order[i]],
            send_sem=place_send.at[i], recv_sem=place_recv.at[order[i]],
            device_id=(order[i], now), device_id_type=MESH,
        ).wait_recv()

    weigh(0, places[me][0:3])

    @pl.when(has_before)
    def _():
        edge_copy(1, now - 1).wait_recv()

    @pl.when(has_after)
    def _():
        edge_copy(0, now + 1).wait_recv()

    @pl.when(jnp.logical_not(has_before))
    def _():
        edge_in[1] = jnp.zeros((8, points), F32)

    @pl.when(jnp.logical_not(has_after))
    def _():
        edge_in[0] = jnp.zeros((8, points), F32)

    row = lax.broadcasted_iota(jnp.int32, (steps, points), 0)
    rates = []
    for k in range(4):
        mine = flux[k]
        later = jnp.where(row == steps - 1, edge_in[0, k : k + 1, :], pltpu.roll(mine, steps - 1, 0))
        earlier = jnp.where(row == 0, edge_in[1, k : k + 1, :], pltpu.roll(mine, 1, 0))
        rates.append(0.5 * (later - earlier))
    mass_rate[...] = rates[0].astype(BF16)
    steady_rate[:, :points] = with_projection(rates[1:])

    for i in range(groups):
        group = order[i]
        slot = i % 2
        if i + 1 < groups:
            await_places(i + 1)
            weigh(1 - slot, places[order[i + 1]][0:3])
        group_places = places[group][0:3]
        by_mass = jnp.dot(mass_rate[...], w_mass[slot], preferred_element_type=F32)
        by_load = jnp.dot(steady_rate[...], w_load[slot], preferred_element_type=F32)
        total = jnp.zeros((steps + TAIL, width), F32)
        for j in range(LAGS):
            columns = slice(j * width, (j + 1) * width)
            piece = by_mass[:, columns] + by_load[3 * steps :, columns]
            for k in range(3):
                piece = piece + by_load[k * steps : (k + 1) * steps, columns] * group_places[k : k + 1]
            piece = jnp.concatenate([piece, jnp.zeros((TAIL, width), F32)], axis=0)
            total = total + (pltpu.roll(piece, j, 0) if j else piece)
        sent[group] = total
        if i > 0:
            part_copy(i, group, 0).start()
        else:
            landed[0, me, steps : 2 * steps, :] = total[:steps]

        @pl.when(has_after)
        def _():
            part_copy(i, group, 1).start()

    def arrived(later, block):
        count = steps + TAIL * later
        return pltpu.make_async_remote_copy(
            src_ref=sent.at[0, pl.ds(0, count), :],
            dst_ref=landed.at[later, block, pl.ds(steps, count), :],
            send_sem=part_send.at[later, 0], recv_sem=part_recv.at[later, block],
            device_id=(order[1], now), device_id_type=MESH,
        )

    for i in range(1, groups):
        arrived(0, order[i]).wait_recv()

    @pl.when(has_before)
    def _():
        for i in range(groups):
            arrived(1, order[i]).wait_recv()

    result = jnp.zeros((steps, width), F32)
    for block in range(groups):
        offset = band[me, block]
        result = result + landed[0, block, pl.ds(steps - offset, steps), :]
        result = result + landed[1, block, pl.ds(2 * steps - offset, steps), :]
    out_ref[...] = result

    for i in range(1, groups):
        place_copy(i).wait_send()
        part_copy(i, order[i], 0).wait_send()

    @pl.when(has_before)
    def _():
        edge_copy(0, now - 1).wait_send()

    @pl.when(has_after)
    def _():
        edge_copy(1, now + 1).wait_send()
        for i in range(groups):
            part_copy(i, order[i], 1).wait_send()


def solution(mesh):
    groups = mesh.shape["obs"]
    blocks = mesh.shape["tm"]

    def local(flow, point_pos, area_vec, observer_angles, band_offset):
        steps, points = flow.shape[1:]
        width = observer_angles.shape[1]
        any_spec = pl.BlockSpec(memory_space=pl.ANY)
        dma = pltpu.SemaphoreType.DMA
        return pl.pallas_call(
            functools.partial(kernel, groups, blocks),
            out_shape=jax.ShapeDtypeStruct((steps, width), F32),
            in_specs=[any_spec] * 5,
            out_specs=pl.BlockSpec(memory_space=pltpu.VMEM),
            scratch_shapes=[
                pltpu.VMEM(flow.shape, F32),
                pltpu.VMEM(point_pos.shape, F32),
                pltpu.VMEM(area_vec.shape, F32),
                pltpu.VMEM(observer_angles.shape, F32),
                pltpu.SMEM(band_offset.shape, jnp.int32),
                pltpu.VMEM((groups, 8, width), F32),
                pltpu.VMEM((2, 8, points), F32),
                pltpu.VMEM((2, 8, points), F32),
                pltpu.VMEM((4, steps, points), F32),
                pltpu.VMEM((4 * steps, 2 * points), BF16),
                pltpu.VMEM((steps, points), BF16),
                pltpu.VMEM((2, points, LAGS * width), BF16),
                pltpu.VMEM((2, 2 * points, LAGS * width), BF16),
                pltpu.VMEM((groups, steps + TAIL, width), F32),
                pltpu.VMEM((2, groups, 3 * steps, width), F32),
                dma((5,)),
                dma((groups,)),
                dma((groups,)),
                dma((2,)),
                dma((2,)),
                dma((2, groups)),
                dma((2, groups)),
            ],
            compiler_params=pltpu.CompilerParams(
                collective_id=0, has_side_effects=True, vmem_limit_bytes=40 * 1024 * 1024
            ),
        )(
            *[
                pltpu.with_memory_space_constraint(x, pltpu.HBM)
                for x in (flow, point_pos, area_vec, observer_angles, band_offset)
            ]
        )

    in_specs = (P(None, "tm", "obs"), P(None, "obs"), P(None, "obs"), P(None, "obs"), P())
    return jax.shard_map(
        local, mesh=mesh, in_specs=in_specs, out_specs=P("tm", "obs"), check_vma=False
    )
```

```python
import functools
import math

import jax
import jax.numpy as jnp
from jax import lax
from jax.experimental import pallas as pl
from jax.experimental.pallas import tpu as pltpu
from jax.sharding import PartitionSpec as P

LAGS = 4
FOUR_PI = 4.0 * math.pi
NEAR_RANGE = 3.25
SOUND_STEP = 1.17
SPHERE_RADIUS = 5.0
MESH = pl.DeviceIdType.MESH
F32 = jnp.float32
BF16 = jnp.bfloat16
TAIL = 8
CHUNK = 64


def split3(x):
    high = x.astype(BF16).astype(F32)
    rest = x - high
    mid = rest.astype(BF16).astype(F32)
    low = (rest - mid).astype(BF16).astype(F32)
    return high, mid, low


def squares(x):
    return x[0:1] * x[0:1] + x[1:2] * x[1:2] + x[2:3] * x[2:3]


def point_factors(points):
    scaled = FOUR_PI * points
    high, mid, low = split3(scaled)
    s_high, s_mid, s_low = split3(squares(scaled))
    ones = jnp.ones((3, points.shape[1]), F32)
    pad = jnp.zeros((8, points.shape[1]), F32)
    rows = [high, high, mid, high, low, mid, s_high, s_mid, s_low, ones, pad]
    return jnp.concatenate(rows, axis=0)


def observer_factors(places):
    scaled = FOUR_PI * places
    high, mid, low = split3(-2.0 * scaled)
    s_high, s_mid, s_low = split3(squares(scaled))
    ones = jnp.ones((3, places.shape[1]), F32)
    pad = jnp.zeros((8, places.shape[1]), F32)
    rows = [high, mid, high, low, high, mid, ones, s_high, s_mid, s_low, pad]
    return jnp.concatenate(rows, axis=0)


def sine_cosine(x):
    turns = jnp.floor(x * (2.0 / math.pi) + 0.5)
    r = ((x - turns * 1.5703125) - turns * 4.8351287841796875e-4) - turns * 3.13855707645416259e-07
    r2 = r * r
    sine = r + r * r2 * (-1.6666654611e-1 + r2 * (8.3321608736e-3 + r2 * -1.9515295891e-4))
    cosine = (1.0 - 0.5 * r2) + r2 * r2 * (
        4.166664568298827e-2 + r2 * (-1.388731625493765e-3 + r2 * 2.443315711809948e-5)
    )
    quadrant = turns.astype(jnp.int32) & 3
    odd = (quadrant & 1) == 1
    first = jnp.where(odd, cosine, sine)
    second = jnp.where(odd, sine, cosine)
    sine = jnp.where(quadrant >= 2, -first, first)
    cosine = jnp.where((quadrant == 1) | (quadrant == 2), -second, second)
    return sine, cosine


def fluxes(flow, area):
    density = 1.0 + 0.2 * flow[0]
    velocity = [0.4 * flow[1 + i] for i in range(3)]
    normal = velocity[0] * area[0:1] + velocity[1] * area[1:2] + velocity[2] * area[2:3]
    mass = density * normal
    return [mass] + [flow[4] * area[i : i + 1] + density * velocity[i] * normal for i in range(3)]


def kernel(
    groups, blocks,
    flow_hbm, pos_hbm, area_hbm, angles_hbm, band_hbm, out_ref,
    flow, pos, area, angles, band, places, edge_out, edge_in, flux, steady_rate, mass_rate,
    w_mass, w_load, sent, landed,
    in_sem, place_send, place_recv, edge_send, edge_recv, part_send, part_recv,
):
    me = lax.axis_index("obs")
    now = lax.axis_index("tm")
    steps = flow.shape[1]
    points = flow.shape[2]
    side = math.isqrt(groups)
    if side * side != groups:
        side = groups
    high, low = me // side, lax.rem(me, side)
    shifts = [(i, j) for i in range(groups // side) for j in range(side)]
    shifts.sort(key=lambda pair: (pair == (0, 0), -min(pair), -sum(pair)))
    peers = range(groups - 1)
    order = [
        lax.rem(high + i, groups // side) * side + lax.rem(low + j, side) for i, j in shifts
    ]
    has_before = now > 0
    has_after = now < blocks - 1

    barrier = pltpu.get_barrier_semaphore()

    def greet(group, block):
        pl.semaphore_signal(barrier, inc=1, device_id=(group, block), device_id_type=MESH)

    for i in peers:
        greet(order[i], now)

    @pl.when(has_before)
    def _():
        greet(me, now - 1)

    @pl.when(has_after)
    def _():
        greet(me, now + 1)

    loads = [
        pltpu.make_async_copy(source, target, in_sem.at[i])
        for i, (source, target) in enumerate(
            [(angles_hbm, angles), (flow_hbm, flow), (area_hbm, area), (pos_hbm, pos), (band_hbm, band)]
        )
    ]
    for load in loads:
        load.start()

    loads[0].wait()
    width = angles.shape[1]
    sine, cosine = sine_cosine(angles[...])
    cos_e = cosine[1:2]
    places[me] = jnp.concatenate(
        [
            SPHERE_RADIUS * (cosine[0:1] * cos_e),
            SPHERE_RADIUS * (sine[0:1] * cos_e),
            SPHERE_RADIUS * sine[1:2],
            jnp.zeros((5, width), F32),
        ],
        axis=0,
    )

    neighbours = jnp.minimum(now, 1) + jnp.minimum(blocks - 1 - now, 1)
    pl.semaphore_wait(barrier, groups - 1 + neighbours)

    def place_copy(i):
        return pltpu.make_async_remote_copy(
            src_ref=places.at[me], dst_ref=places.at[me],
            send_sem=place_send.at[i], recv_sem=place_recv.at[me],
            device_id=(order[i], now), device_id_type=MESH,
        )

    for i in peers:
        place_copy(i).start()

    loads[1].wait()
    loads[2].wait()
    area_rows = area[...]
    whole = fluxes(flow, area_rows)
    for k in range(4):
        flux[k] = whole[k]
    edge_pad = jnp.zeros((4, points), F32)
    edge_out[0] = jnp.concatenate([flux[k, 0:1, :] for k in range(4)] + [edge_pad], axis=0)
    edge_out[1] = jnp.concatenate(
        [flux[k, steps - 1 : steps, :] for k in range(4)] + [edge_pad], axis=0
    )

    def edge_copy(side, block):
        return pltpu.make_async_remote_copy(
            src_ref=edge_out.at[side], dst_ref=edge_in.at[side],
            send_sem=edge_send.at[side], recv_sem=edge_recv.at[side],
            device_id=(me, block), device_id_type=MESH,
        )

    @pl.when(has_before)
    def _():
        edge_copy(0, now - 1).start()

    @pl.when(has_after)
    def _():
        edge_copy(1, now + 1).start()

    for j in range(2):
        for b in range(groups):
            landed[j, b, 0:steps, :] = jnp.zeros((steps, width), F32)
            landed[j, b, 2 * steps + TAIL :, :] = jnp.zeros((steps - TAIL, width), F32)

    @pl.when(jnp.logical_not(has_before))
    def _():
        for b in range(groups):
            landed[1, b, steps : 2 * steps + TAIL, :] = jnp.zeros((steps + TAIL, width), F32)

    loads[3].wait()
    loads[4].wait()
    spots = pos[...]
    factors = jnp.transpose(point_factors(spots)).astype(BF16)
    spot_rows = [spots[i : i + 1, :] for i in range(3)]

    def with_projection(parts):
        rounded = [part.astype(BF16) for part in parts]
        wide = [part.astype(F32) for part in rounded]
        along = wide[0] * spot_rows[0] + wide[1] * spot_rows[1] + wide[2] * spot_rows[2]
        return jnp.concatenate(rounded + [(-along).astype(BF16)], axis=0)

    steady_rate[:, points:] = with_projection([flux[1 + k] for k in range(3)])

    near = 1.0 / (SOUND_STEP * FOUR_PI)
    slope = NEAR_RANGE / SOUND_STEP

    def weigh(slot, group_places):
        squared = jnp.dot(
            factors, observer_factors(group_places).astype(BF16), preferred_element_type=F32
        )
        for start in range(0, points, CHUNK):
            rows = slice(start, start + CHUNK)
            load_rows = slice(points + start, points + start + CHUNK)
            r = lax.rsqrt(squared[rows])
            u = near - slope * r
            z = u - r
            y = z - r
            tents = [
                jnp.maximum(0.0, -z),
                jnp.maximum(0.0, jnp.minimum(u, -y)),
                jnp.maximum(0.0, jnp.minimum(z, r - y)),
                jnp.maximum(0.0, y),
            ]
            by_rate = r * (FOUR_PI / SOUND_STEP)
            by_load = r * r * (FOUR_PI * FOUR_PI)
            for j in range(LAGS):
                columns = slice(j * width, (j + 1) * width)
                w_mass[slot, rows, columns] = tents[j].astype(BF16)
                w_load[slot, rows, columns] = (tents[j] * by_rate).astype(BF16)
                w_load[slot, load_rows, columns] = (tents[j] * by_load).astype(BF16)

    def part_copy(i, group, later):
        count = steps + TAIL * later
        return pltpu.make_async_remote_copy(
            src_ref=sent.at[group, pl.ds(0, count), :],
            dst_ref=landed.at[later, me, pl.ds(steps, count), :],
            send_sem=part_send.at[later, i], recv_sem=part_recv.at[later, me],
            device_id=(group, now + later), device_id_type=MESH,
        )

    def await_places(i):
        pltpu.make_async_remote_copy(
            src_ref=places.at[order[i]], dst_ref=places.at[order[i]],
            send_sem=place_send.at[i], recv_sem=place_recv.at[order[i]],
            device_id=(order[i], now), device_id_type=MESH,
        ).wait_recv()

    if groups > 1:
        await_places(0)
    weigh(0, places[order[0]][0:3])

    @pl.when(has_before)
    def _():
        edge_copy(1, now - 1).wait_recv()

    @pl.when(has_after)
    def _():
        edge_copy(0, now + 1).wait_recv()

    @pl.when(jnp.logical_not(has_before))
    def _():
        edge_in[1] = jnp.zeros((8, points), F32)

    @pl.when(jnp.logical_not(has_after))
    def _():
        edge_in[0] = jnp.zeros((8, points), F32)

    row = lax.broadcasted_iota(jnp.int32, (steps, points), 0)
    rates = []
    for k in range(4):
        mine = flux[k]
        later = jnp.where(row == steps - 1, edge_in[0, k : k + 1, :], pltpu.roll(mine, steps - 1, 0))
        earlier = jnp.where(row == 0, edge_in[1, k : k + 1, :], pltpu.roll(mine, 1, 0))
        rates.append(0.5 * (later - earlier))
    mass_rate[...] = rates[0].astype(BF16)
    steady_rate[:, :points] = with_projection(rates[1:])

    for i in range(groups):
        group = order[i]
        slot = i % 2
        if i + 1 < groups:
            if i + 1 in peers:
                await_places(i + 1)
            weigh(1 - slot, places[order[i + 1]][0:3])
        group_places = places[group][0:3]
        by_mass = jnp.dot(mass_rate[...], w_mass[slot], preferred_element_type=F32)
        by_load = jnp.dot(steady_rate[...], w_load[slot], preferred_element_type=F32)
        total = jnp.zeros((steps + TAIL, width), F32)
        for j in range(LAGS):
            columns = slice(j * width, (j + 1) * width)
            piece = by_mass[:, columns] + by_load[3 * steps :, columns]
            for k in range(3):
                piece = piece + by_load[k * steps : (k + 1) * steps, columns] * group_places[k : k + 1]
            piece = jnp.concatenate([piece, jnp.zeros((TAIL, width), F32)], axis=0)
            total = total + (pltpu.roll(piece, j, 0) if j else piece)
        sent[group] = total
        if i in peers:
            part_copy(i, group, 0).start()
        else:
            landed[0, me, steps : 2 * steps, :] = total[:steps]

        @pl.when(has_after)
        def _():
            part_copy(i, group, 1).start()

    def arrived(later, block):
        count = steps + TAIL * later
        return pltpu.make_async_remote_copy(
            src_ref=sent.at[0, pl.ds(0, count), :],
            dst_ref=landed.at[later, block, pl.ds(steps, count), :],
            send_sem=part_send.at[later, 0], recv_sem=part_recv.at[later, block],
            device_id=(order[0], now), device_id_type=MESH,
        )

    for i in peers:
        arrived(0, order[i]).wait_recv()

    @pl.when(has_before)
    def _():
        for i in range(groups):
            arrived(1, order[i]).wait_recv()

    result = jnp.zeros((steps, width), F32)
    for block in range(groups):
        offset = band[me, block]
        result = result + landed[0, block, pl.ds(steps - offset, steps), :]
        result = result + landed[1, block, pl.ds(2 * steps - offset, steps), :]
    out_ref[...] = result

    for i in peers:
        place_copy(i).wait_send()
        part_copy(i, order[i], 0).wait_send()

    @pl.when(has_before)
    def _():
        edge_copy(0, now - 1).wait_send()

    @pl.when(has_after)
    def _():
        edge_copy(1, now + 1).wait_send()
        for i in range(groups):
            part_copy(i, order[i], 1).wait_send()


def solution(mesh):
    groups = mesh.shape["obs"]
    blocks = mesh.shape["tm"]

    def local(flow, point_pos, area_vec, observer_angles, band_offset):
        steps, points = flow.shape[1:]
        width = observer_angles.shape[1]
        any_spec = pl.BlockSpec(memory_space=pl.ANY)
        dma = pltpu.SemaphoreType.DMA
        return pl.pallas_call(
            functools.partial(kernel, groups, blocks),
            out_shape=jax.ShapeDtypeStruct((steps, width), F32),
            in_specs=[any_spec] * 5,
            out_specs=pl.BlockSpec(memory_space=pltpu.VMEM),
            scratch_shapes=[
                pltpu.VMEM(flow.shape, F32),
                pltpu.VMEM(point_pos.shape, F32),
                pltpu.VMEM(area_vec.shape, F32),
                pltpu.VMEM(observer_angles.shape, F32),
                pltpu.SMEM(band_offset.shape, jnp.int32),
                pltpu.VMEM((groups, 8, width), F32),
                pltpu.VMEM((2, 8, points), F32),
                pltpu.VMEM((2, 8, points), F32),
                pltpu.VMEM((4, steps, points), F32),
                pltpu.VMEM((4 * steps, 2 * points), BF16),
                pltpu.VMEM((steps, points), BF16),
                pltpu.VMEM((2, points, LAGS * width), BF16),
                pltpu.VMEM((2, 2 * points, LAGS * width), BF16),
                pltpu.VMEM((groups, steps + TAIL, width), F32),
                pltpu.VMEM((2, groups, 3 * steps, width), F32),
                dma((5,)),
                dma((groups,)),
                dma((groups,)),
                dma((2,)),
                dma((2,)),
                dma((2, groups)),
                dma((2, groups)),
            ],
            compiler_params=pltpu.CompilerParams(
                collective_id=0, has_side_effects=True, vmem_limit_bytes=40 * 1024 * 1024
            ),
        )(
            *[
                pltpu.with_memory_space_constraint(x, pltpu.HBM)
                for x in (flow, point_pos, area_vec, observer_angles, band_offset)
            ]
        )

    in_specs = (P(None, "tm", "obs"), P(None, "obs"), P(None, "obs"), P(None, "obs"), P())
    return jax.shard_map(
        local, mesh=mesh, in_specs=in_specs, out_specs=P("tm", "obs"), check_vma=False
    )
```

```python
import functools
import math

import jax
import jax.numpy as jnp
from jax import lax
from jax.experimental import pallas as pl
from jax.experimental.pallas import tpu as pltpu
from jax.sharding import PartitionSpec as P

LAGS = 4
FOUR_PI = 4.0 * math.pi
NEAR_RANGE = 3.25
SOUND_STEP = 1.17
SPHERE_RADIUS = 5.0
MESH = pl.DeviceIdType.MESH
F32 = jnp.float32
BF16 = jnp.bfloat16
TAIL = 8
CHUNK = 16


def split3(x):
    high = x.astype(BF16).astype(F32)
    rest = x - high
    mid = rest.astype(BF16).astype(F32)
    low = (rest - mid).astype(BF16).astype(F32)
    return high, mid, low


def squares(x):
    return x[0:1] * x[0:1] + x[1:2] * x[1:2] + x[2:3] * x[2:3]


def point_factors(points):
    scaled = FOUR_PI * points
    high, mid, low = split3(scaled)
    s_high, s_mid, s_low = split3(squares(scaled))
    ones = jnp.ones((3, points.shape[1]), F32)
    pad = jnp.zeros((8, points.shape[1]), F32)
    rows = [high, high, mid, high, low, mid, s_high, s_mid, s_low, ones, pad]
    return jnp.concatenate(rows, axis=0)


def observer_factors(places):
    scaled = FOUR_PI * places
    high, mid, low = split3(-2.0 * scaled)
    s_high, s_mid, s_low = split3(squares(scaled))
    ones = jnp.ones((3, places.shape[1]), F32)
    pad = jnp.zeros((8, places.shape[1]), F32)
    rows = [high, mid, high, low, high, mid, ones, s_high, s_mid, s_low, pad]
    return jnp.concatenate(rows, axis=0)


def sine_cosine(x):
    turns = jnp.floor(x * (2.0 / math.pi) + 0.5)
    r = ((x - turns * 1.5703125) - turns * 4.8351287841796875e-4) - turns * 3.13855707645416259e-07
    r2 = r * r
    sine = r + r * r2 * (-1.6666654611e-1 + r2 * (8.3321608736e-3 + r2 * -1.9515295891e-4))
    cosine = (1.0 - 0.5 * r2) + r2 * r2 * (
        4.166664568298827e-2 + r2 * (-1.388731625493765e-3 + r2 * 2.443315711809948e-5)
    )
    quadrant = turns.astype(jnp.int32) & 3
    odd = (quadrant & 1) == 1
    first = jnp.where(odd, cosine, sine)
    second = jnp.where(odd, sine, cosine)
    sine = jnp.where(quadrant >= 2, -first, first)
    cosine = jnp.where((quadrant == 1) | (quadrant == 2), -second, second)
    return sine, cosine


def fluxes(flow, area):
    density = 1.0 + 0.2 * flow[0]
    velocity = [0.4 * flow[1 + i] for i in range(3)]
    normal = velocity[0] * area[0:1] + velocity[1] * area[1:2] + velocity[2] * area[2:3]
    mass = density * normal
    return [mass] + [flow[4] * area[i : i + 1] + density * velocity[i] * normal for i in range(3)]


def kernel(
    groups, blocks,
    flow_hbm, pos_hbm, area_hbm, angles_hbm, band_hbm, out_ref,
    flow, pos, area, angles, band, places, edge_out, edge_in, flux, steady_rate, mass_rate,
    w_mass, w_load, sent, landed,
    in_sem, place_send, place_recv, edge_send, edge_recv, part_send, part_recv,
):
    me = lax.axis_index("obs")
    now = lax.axis_index("tm")
    steps = flow.shape[1]
    points = flow.shape[2]
    side = math.isqrt(groups)
    if side * side != groups:
        side = groups
    high, low = me // side, lax.rem(me, side)
    shifts = [(i, j) for i in range(groups // side) for j in range(side)]
    shifts.sort(key=lambda pair: (pair == (0, 0), -min(pair), -sum(pair)))
    peers = range(groups - 1)
    order = [
        lax.rem(high + i, groups // side) * side + lax.rem(low + j, side) for i, j in shifts
    ]
    has_before = now > 0
    has_after = now < blocks - 1

    barrier = pltpu.get_barrier_semaphore()

    def greet(group, block):
        pl.semaphore_signal(barrier, inc=1, device_id=(group, block), device_id_type=MESH)

    for i in peers:
        greet(order[i], now)

    @pl.when(has_before)
    def _():
        greet(me, now - 1)

    @pl.when(has_after)
    def _():
        greet(me, now + 1)

    loads = [
        pltpu.make_async_copy(source, target, in_sem.at[i])
        for i, (source, target) in enumerate(
            [(angles_hbm, angles), (flow_hbm, flow), (area_hbm, area), (pos_hbm, pos), (band_hbm, band)]
        )
    ]
    for load in loads:
        load.start()

    loads[0].wait()
    width = angles.shape[1]
    sine, cosine = sine_cosine(angles[...])
    cos_e = cosine[1:2]
    places[me] = jnp.concatenate(
        [
            SPHERE_RADIUS * (cosine[0:1] * cos_e),
            SPHERE_RADIUS * (sine[0:1] * cos_e),
            SPHERE_RADIUS * sine[1:2],
            jnp.zeros((5, width), F32),
        ],
        axis=0,
    )

    neighbours = jnp.minimum(now, 1) + jnp.minimum(blocks - 1 - now, 1)
    pl.semaphore_wait(barrier, groups - 1 + neighbours)

    def place_copy(i):
        return pltpu.make_async_remote_copy(
            src_ref=places.at[me], dst_ref=places.at[me],
            send_sem=place_send.at[i], recv_sem=place_recv.at[me],
            device_id=(order[i], now), device_id_type=MESH,
        )

    for i in peers:
        place_copy(i).start()

    loads[1].wait()
    loads[2].wait()
    area_rows = area[...]
    whole = fluxes(flow, area_rows)
    for k in range(4):
        flux[k] = whole[k]
    edge_pad = jnp.zeros((4, points), F32)
    edge_out[0] = jnp.concatenate([flux[k, 0:1, :] for k in range(4)] + [edge_pad], axis=0)
    edge_out[1] = jnp.concatenate(
        [flux[k, steps - 1 : steps, :] for k in range(4)] + [edge_pad], axis=0
    )

    def edge_copy(side, block):
        return pltpu.make_async_remote_copy(
            src_ref=edge_out.at[side], dst_ref=edge_in.at[side],
            send_sem=edge_send.at[side], recv_sem=edge_recv.at[side],
            device_id=(me, block), device_id_type=MESH,
        )

    @pl.when(has_before)
    def _():
        edge_copy(0, now - 1).start()

    @pl.when(has_after)
    def _():
        edge_copy(1, now + 1).start()

    for j in range(2):
        for b in range(groups):
            landed[j, b, 0:steps, :] = jnp.zeros((steps, width), F32)
            landed[j, b, 2 * steps + TAIL :, :] = jnp.zeros((steps - TAIL, width), F32)

    @pl.when(jnp.logical_not(has_before))
    def _():
        for b in range(groups):
            landed[1, b, steps : 2 * steps + TAIL, :] = jnp.zeros((steps + TAIL, width), F32)

    loads[3].wait()
    loads[4].wait()
    spots = pos[...]
    factors = point_factors(spots).astype(BF16)
    spot_rows = [spots[i : i + 1, :] for i in range(3)]

    def with_projection(parts):
        rounded = [part.astype(BF16) for part in parts]
        wide = [part.astype(F32) for part in rounded]
        along = wide[0] * spot_rows[0] + wide[1] * spot_rows[1] + wide[2] * spot_rows[2]
        return jnp.concatenate(rounded + [(-along).astype(BF16)], axis=0)

    steady_rate[:, points:] = with_projection([flux[1 + k] for k in range(3)])

    near = 1.0 / (SOUND_STEP * FOUR_PI)
    slope = NEAR_RANGE / SOUND_STEP

    def weigh(slot, group_places):
        watchers = jnp.transpose(observer_factors(group_places)).astype(BF16)
        squared = jnp.dot(watchers, factors, preferred_element_type=F32)
        for start in range(0, width, CHUNK):
            rows = slice(start, start + CHUNK)
            r = lax.rsqrt(squared[rows])
            u = near - slope * r
            z = u - r
            y = z - r
            tents = [
                jnp.maximum(0.0, -z),
                jnp.maximum(0.0, jnp.minimum(u, -y)),
                jnp.maximum(0.0, jnp.minimum(z, r - y)),
                jnp.maximum(0.0, y),
            ]
            by_rate = r * (FOUR_PI / SOUND_STEP)
            by_load = r * r * (FOUR_PI * FOUR_PI)
            for j in range(LAGS):
                lag_rows = slice(j * width + start, j * width + start + CHUNK)
                w_mass[slot, lag_rows, :] = tents[j].astype(BF16)
                w_load[slot, lag_rows, :points] = (tents[j] * by_rate).astype(BF16)
                w_load[slot, lag_rows, points:] = (tents[j] * by_load).astype(BF16)

    def part_copy(i, group, later):
        count = steps + TAIL * later
        return pltpu.make_async_remote_copy(
            src_ref=sent.at[group, pl.ds(0, count), :],
            dst_ref=landed.at[later, me, pl.ds(steps, count), :],
            send_sem=part_send.at[later, i], recv_sem=part_recv.at[later, me],
            device_id=(group, now + later), device_id_type=MESH,
        )

    def await_places(i):
        pltpu.make_async_remote_copy(
            src_ref=places.at[order[i]], dst_ref=places.at[order[i]],
            send_sem=place_send.at[i], recv_sem=place_recv.at[order[i]],
            device_id=(order[i], now), device_id_type=MESH,
        ).wait_recv()

    if groups > 1:
        await_places(0)
    weigh(0, places[order[0]][0:3])

    @pl.when(has_before)
    def _():
        edge_copy(1, now - 1).wait_recv()

    @pl.when(has_after)
    def _():
        edge_copy(0, now + 1).wait_recv()

    @pl.when(jnp.logical_not(has_before))
    def _():
        edge_in[1] = jnp.zeros((8, points), F32)

    @pl.when(jnp.logical_not(has_after))
    def _():
        edge_in[0] = jnp.zeros((8, points), F32)

    row = lax.broadcasted_iota(jnp.int32, (steps, points), 0)
    rates = []
    for k in range(4):
        mine = flux[k]
        later = jnp.where(row == steps - 1, edge_in[0, k : k + 1, :], pltpu.roll(mine, steps - 1, 0))
        earlier = jnp.where(row == 0, edge_in[1, k : k + 1, :], pltpu.roll(mine, 1, 0))
        rates.append(0.5 * (later - earlier))
    mass_rate[:steps] = rates[0].astype(BF16)
    mass_rate[steps:] = jnp.zeros((steps, points), BF16)
    steady_rate[:, :points] = with_projection(rates[1:])

    for i in range(groups):
        group = order[i]
        slot = i % 2
        if i + 1 < groups:
            if i + 1 in peers:
                await_places(i + 1)
            weigh(1 - slot, places[order[i + 1]][0:3])
        turned = jnp.transpose(places[group])
        lane = lax.broadcasted_iota(jnp.int32, (width, 2 * steps), 1)
        front = lane < steps
        scale_low = jnp.where(front, turned[:, 0:1], turned[:, 1:2])
        scale_high = jnp.where(front, turned[:, 2:3], 1.0)
        across = (((1,), (1,)), ((), ()))
        by_mass = lax.dot_general(
            w_mass[slot], mass_rate[...], across, preferred_element_type=F32
        )
        by_load = lax.dot_general(
            w_load[slot], steady_rate[...], across, preferred_element_type=F32
        )
        total = jnp.zeros((width, 2 * steps), F32)
        for j in range(LAGS):
            rows = slice(j * width, (j + 1) * width)
            piece = by_mass[rows] + by_load[rows, : 2 * steps] * scale_low
            piece = piece + by_load[rows, 2 * steps :] * scale_high
            piece = jnp.where(front, piece + pltpu.roll(piece, steps, 1), 0.0)
            total = total + (pltpu.roll(piece, j, 1) if j else piece)
        total = jnp.transpose(total)[: steps + TAIL]
        sent[group] = total
        if i in peers:
            part_copy(i, group, 0).start()
        else:
            landed[0, me, steps : 2 * steps, :] = total[:steps]

        @pl.when(has_after)
        def _():
            part_copy(i, group, 1).start()

    def arrived(later, block):
        count = steps + TAIL * later
        return pltpu.make_async_remote_copy(
            src_ref=sent.at[0, pl.ds(0, count), :],
            dst_ref=landed.at[later, block, pl.ds(steps, count), :],
            send_sem=part_send.at[later, 0], recv_sem=part_recv.at[later, block],
            device_id=(order[0], now), device_id_type=MESH,
        )

    for i in peers:
        arrived(0, order[i]).wait_recv()

    @pl.when(has_before)
    def _():
        for i in range(groups):
            arrived(1, order[i]).wait_recv()

    result = jnp.zeros((steps, width), F32)
    for block in range(groups):
        offset = band[me, block]
        result = result + landed[0, block, pl.ds(steps - offset, steps), :]
        result = result + landed[1, block, pl.ds(2 * steps - offset, steps), :]
    out_ref[...] = result

    for i in peers:
        place_copy(i).wait_send()
        part_copy(i, order[i], 0).wait_send()

    @pl.when(has_before)
    def _():
        edge_copy(0, now - 1).wait_send()

    @pl.when(has_after)
    def _():
        edge_copy(1, now + 1).wait_send()
        for i in range(groups):
            part_copy(i, order[i], 1).wait_send()


def solution(mesh):
    groups = mesh.shape["obs"]
    blocks = mesh.shape["tm"]

    def local(flow, point_pos, area_vec, observer_angles, band_offset):
        steps, points = flow.shape[1:]
        width = observer_angles.shape[1]
        any_spec = pl.BlockSpec(memory_space=pl.ANY)
        dma = pltpu.SemaphoreType.DMA
        return pl.pallas_call(
            functools.partial(kernel, groups, blocks),
            out_shape=jax.ShapeDtypeStruct((steps, width), F32),
            in_specs=[any_spec] * 5,
            out_specs=pl.BlockSpec(memory_space=pltpu.VMEM),
            scratch_shapes=[
                pltpu.VMEM(flow.shape, F32),
                pltpu.VMEM(point_pos.shape, F32),
                pltpu.VMEM(area_vec.shape, F32),
                pltpu.VMEM(observer_angles.shape, F32),
                pltpu.SMEM(band_offset.shape, jnp.int32),
                pltpu.VMEM((groups, 8, width), F32),
                pltpu.VMEM((2, 8, points), F32),
                pltpu.VMEM((2, 8, points), F32),
                pltpu.VMEM((4, steps, points), F32),
                pltpu.VMEM((4 * steps, 2 * points), BF16),
                pltpu.VMEM((2 * steps, points), BF16),
                pltpu.VMEM((2, LAGS * width, points), BF16),
                pltpu.VMEM((2, LAGS * width, 2 * points), BF16),
                pltpu.VMEM((groups, steps + TAIL, width), F32),
                pltpu.VMEM((2, groups, 3 * steps, width), F32),
                dma((5,)),
                dma((groups,)),
                dma((groups,)),
                dma((2,)),
                dma((2,)),
                dma((2, groups)),
                dma((2, groups)),
            ],
            compiler_params=pltpu.CompilerParams(
                collective_id=0, has_side_effects=True, vmem_limit_bytes=40 * 1024 * 1024
            ),
        )(
            *[
                pltpu.with_memory_space_constraint(x, pltpu.HBM)
                for x in (flow, point_pos, area_vec, observer_angles, band_offset)
            ]
        )

    in_specs = (P(None, "tm", "obs"), P(None, "obs"), P(None, "obs"), P(None, "obs"), P())
    return jax.shard_map(
        local, mesh=mesh, in_specs=in_specs, out_specs=P("tm", "obs"), check_vma=False
    )
```

```python
import functools
import math

import jax
import jax.numpy as jnp
from jax import lax
from jax.experimental import pallas as pl
from jax.experimental.pallas import tpu as pltpu
from jax.sharding import PartitionSpec as P

LAGS = 4
FOUR_PI = 4.0 * math.pi
NEAR_RANGE = 3.25
SOUND_STEP = 1.17
SPHERE_RADIUS = 5.0
MESH = pl.DeviceIdType.MESH
F32 = jnp.float32
BF16 = jnp.bfloat16
TAIL = 8
CHUNK = 64


def split3(x):
    high = x.astype(BF16).astype(F32)
    rest = x - high
    mid = rest.astype(BF16).astype(F32)
    low = (rest - mid).astype(BF16).astype(F32)
    return high, mid, low


def squares(x):
    return x[0:1] * x[0:1] + x[1:2] * x[1:2] + x[2:3] * x[2:3]


def point_factors(points):
    scaled = FOUR_PI * points
    high, mid, low = split3(scaled)
    s_high, s_mid, s_low = split3(squares(scaled))
    ones = jnp.ones((3, points.shape[1]), F32)
    pad = jnp.zeros((8, points.shape[1]), F32)
    rows = [high, high, mid, high, low, mid, s_high, s_mid, s_low, ones, pad]
    return jnp.concatenate(rows, axis=0)


def observer_factors(places):
    scaled = FOUR_PI * places
    high, mid, low = split3(-2.0 * scaled)
    s_high, s_mid, s_low = split3(squares(scaled))
    ones = jnp.ones((3, places.shape[1]), F32)
    pad = jnp.zeros((8, places.shape[1]), F32)
    rows = [high, mid, high, low, high, mid, ones, s_high, s_mid, s_low, pad]
    return jnp.concatenate(rows, axis=0)


def sine_cosine(x):
    turns = jnp.floor(x * (2.0 / math.pi) + 0.5)
    r = ((x - turns * 1.5703125) - turns * 4.8351287841796875e-4) - turns * 3.13855707645416259e-07
    r2 = r * r
    sine = r + r * r2 * (-1.6666654611e-1 + r2 * (8.3321608736e-3 + r2 * -1.9515295891e-4))
    cosine = (1.0 - 0.5 * r2) + r2 * r2 * (
        4.166664568298827e-2 + r2 * (-1.388731625493765e-3 + r2 * 2.443315711809948e-5)
    )
    quadrant = turns.astype(jnp.int32) & 3
    odd = (quadrant & 1) == 1
    first = jnp.where(odd, cosine, sine)
    second = jnp.where(odd, sine, cosine)
    sine = jnp.where(quadrant >= 2, -first, first)
    cosine = jnp.where((quadrant == 1) | (quadrant == 2), -second, second)
    return sine, cosine


def fluxes(flow, area):
    density = 1.0 + 0.2 * flow[0]
    velocity = [0.4 * flow[1 + i] for i in range(3)]
    normal = velocity[0] * area[0:1] + velocity[1] * area[1:2] + velocity[2] * area[2:3]
    mass = density * normal
    return [mass] + [flow[4] * area[i : i + 1] + density * velocity[i] * normal for i in range(3)]


def kernel(
    groups, blocks,
    flow_hbm, pos_hbm, area_hbm, angles_hbm, band_hbm, out_ref,
    flow, pos, area, angles, band, places, edge_out, edge_in, flux, steady_rate, mass_rate,
    w_mass, w_load, sent, landed,
    in_sem, place_send, place_recv, edge_send, edge_recv, part_send, part_recv,
):
    me = lax.axis_index("obs")
    now = lax.axis_index("tm")
    steps = flow.shape[1]
    points = flow.shape[2]
    side = math.isqrt(groups)
    if side * side != groups:
        side = groups
    high, low = me // side, lax.rem(me, side)
    shifts = [(i, j) for i in range(groups // side) for j in range(side)]
    shifts.sort(key=lambda pair: (pair == (0, 0), -min(pair), -sum(pair)))
    peers = range(groups - 1)
    order = [
        lax.rem(high + i, groups // side) * side + lax.rem(low + j, side) for i, j in shifts
    ]
    has_before = now > 0
    has_after = now < blocks - 1

    barrier = pltpu.get_barrier_semaphore()

    def greet(group, block):
        pl.semaphore_signal(barrier, inc=1, device_id=(group, block), device_id_type=MESH)

    for i in peers:
        greet(order[i], now)

    @pl.when(has_before)
    def _():
        greet(me, now - 1)

    @pl.when(has_after)
    def _():
        greet(me, now + 1)

    loads = [
        pltpu.make_async_copy(source, target, in_sem.at[i])
        for i, (source, target) in enumerate(
            [(angles_hbm, angles), (flow_hbm, flow), (area_hbm, area), (pos_hbm, pos), (band_hbm, band)]
        )
    ]
    for load in loads:
        load.start()

    loads[0].wait()
    width = angles.shape[1]
    sine, cosine = sine_cosine(angles[...])
    cos_e = cosine[1:2]
    places[me] = jnp.concatenate(
        [
            SPHERE_RADIUS * (cosine[0:1] * cos_e),
            SPHERE_RADIUS * (sine[0:1] * cos_e),
            SPHERE_RADIUS * sine[1:2],
            jnp.zeros((5, width), F32),
        ],
        axis=0,
    )

    neighbours = jnp.minimum(now, 1) + jnp.minimum(blocks - 1 - now, 1)
    pl.semaphore_wait(barrier, groups - 1 + neighbours)

    def place_copy(i):
        return pltpu.make_async_remote_copy(
            src_ref=places.at[me], dst_ref=places.at[me],
            send_sem=place_send.at[i], recv_sem=place_recv.at[me],
            device_id=(order[i], now), device_id_type=MESH,
        )

    for i in peers:
        place_copy(i).start()

    loads[1].wait()
    loads[2].wait()
    area_rows = area[...]
    edge_pad = jnp.zeros((4, points), F32)
    first = fluxes(flow[:, 0:8, :], area_rows)
    edge_out[0] = jnp.concatenate([part[0:1] for part in first] + [edge_pad], axis=0)
    last = fluxes(flow[:, steps - 8 : steps, :], area_rows)
    edge_out[1] = jnp.concatenate([part[7:8] for part in last] + [edge_pad], axis=0)

    def edge_copy(side, block):
        return pltpu.make_async_remote_copy(
            src_ref=edge_out.at[side], dst_ref=edge_in.at[side],
            send_sem=edge_send.at[side], recv_sem=edge_recv.at[side],
            device_id=(me, block), device_id_type=MESH,
        )

    @pl.when(has_before)
    def _():
        edge_copy(0, now - 1).start()

    @pl.when(has_after)
    def _():
        edge_copy(1, now + 1).start()

    whole = fluxes(flow, area_rows)
    for k in range(4):
        flux[k] = whole[k]

    for j in range(2):
        for b in range(groups):
            landed[j, b, 0:steps, :] = jnp.zeros((steps, width), F32)
            landed[j, b, 2 * steps + TAIL :, :] = jnp.zeros((steps - TAIL, width), F32)

    @pl.when(jnp.logical_not(has_before))
    def _():
        for b in range(groups):
            landed[1, b, steps : 2 * steps + TAIL, :] = jnp.zeros((steps + TAIL, width), F32)

    loads[3].wait()
    loads[4].wait()
    spots = pos[...]
    factors = jnp.transpose(point_factors(spots)).astype(BF16)
    spot_rows = [spots[i : i + 1, :] for i in range(3)]

    def with_projection(parts):
        rounded = [part.astype(BF16) for part in parts]
        wide = [part.astype(F32) for part in rounded]
        along = wide[0] * spot_rows[0] + wide[1] * spot_rows[1] + wide[2] * spot_rows[2]
        return jnp.concatenate(rounded + [(-along).astype(BF16)], axis=0)

    steady_rate[:, points:] = with_projection([flux[1 + k] for k in range(3)])

    near = 1.0 / (SOUND_STEP * FOUR_PI)
    slope = NEAR_RANGE / SOUND_STEP

    def weigh(slot, group_places):
        squared = jnp.dot(
            factors, observer_factors(group_places).astype(BF16), preferred_element_type=F32
        )
        for start in range(0, points, CHUNK):
            rows = slice(start, start + CHUNK)
            load_rows = slice(points + start, points + start + CHUNK)
            r = lax.rsqrt(squared[rows])
            u = near - slope * r
            z = u - r
            y = z - r
            tents = [
                jnp.maximum(0.0, -z),
                jnp.maximum(0.0, jnp.minimum(u, -y)),
                jnp.maximum(0.0, jnp.minimum(z, r - y)),
                jnp.maximum(0.0, y),
            ]
            by_rate = r * (FOUR_PI / SOUND_STEP)
            by_load = r * r * (FOUR_PI * FOUR_PI)
            for j in range(LAGS):
                columns = slice(j * width, (j + 1) * width)
                w_mass[slot, rows, columns] = tents[j].astype(BF16)
                w_load[slot, rows, columns] = (tents[j] * by_rate).astype(BF16)
                w_load[slot, load_rows, columns] = (tents[j] * by_load).astype(BF16)

    def part_copy(i, group, later):
        count = steps + TAIL * later
        return pltpu.make_async_remote_copy(
            src_ref=sent.at[group, pl.ds(0, count), :],
            dst_ref=landed.at[later, me, pl.ds(steps, count), :],
            send_sem=part_send.at[later, i], recv_sem=part_recv.at[later, me],
            device_id=(group, now + later), device_id_type=MESH,
        )

    def await_places(i):
        pltpu.make_async_remote_copy(
            src_ref=places.at[order[i]], dst_ref=places.at[order[i]],
            send_sem=place_send.at[i], recv_sem=place_recv.at[order[i]],
            device_id=(order[i], now), device_id_type=MESH,
        ).wait_recv()

    if groups > 1:
        await_places(0)
    weigh(0, places[order[0]][0:3])

    @pl.when(has_before)
    def _():
        edge_copy(1, now - 1).wait_recv()

    @pl.when(has_after)
    def _():
        edge_copy(0, now + 1).wait_recv()

    @pl.when(jnp.logical_not(has_before))
    def _():
        edge_in[1] = jnp.zeros((8, points), F32)

    @pl.when(jnp.logical_not(has_after))
    def _():
        edge_in[0] = jnp.zeros((8, points), F32)

    row = lax.broadcasted_iota(jnp.int32, (steps, points), 0)
    rates = []
    for k in range(4):
        mine = flux[k]
        later = jnp.where(row == steps - 1, edge_in[0, k : k + 1, :], pltpu.roll(mine, steps - 1, 0))
        earlier = jnp.where(row == 0, edge_in[1, k : k + 1, :], pltpu.roll(mine, 1, 0))
        rates.append(0.5 * (later - earlier))
    mass_rate[...] = rates[0].astype(BF16)
    steady_rate[:, :points] = with_projection(rates[1:])

    for i in range(groups):
        group = order[i]
        slot = i % 2
        if i + 1 < groups:
            if i + 1 in peers:
                await_places(i + 1)
            weigh(1 - slot, places[order[i + 1]][0:3])
        group_places = places[group][0:3]
        by_mass = jnp.dot(mass_rate[...], w_mass[slot], preferred_element_type=F32)
        by_load = jnp.dot(steady_rate[...], w_load[slot], preferred_element_type=F32)
        total = jnp.zeros((steps + TAIL, width), F32)
        for j in range(LAGS):
            columns = slice(j * width, (j + 1) * width)
            piece = by_mass[:, columns] + by_load[3 * steps :, columns]
            for k in range(3):
                piece = piece + by_load[k * steps : (k + 1) * steps, columns] * group_places[k : k + 1]
            piece = jnp.concatenate([piece, jnp.zeros((TAIL, width), F32)], axis=0)
            total = total + (pltpu.roll(piece, j, 0) if j else piece)
        sent[group] = total
        if i in peers:
            part_copy(i, group, 0).start()
        else:
            landed[0, me, steps : 2 * steps, :] = total[:steps]

        @pl.when(has_after)
        def _():
            part_copy(i, group, 1).start()

    def arrived(later, block):
        count = steps + TAIL * later
        return pltpu.make_async_remote_copy(
            src_ref=sent.at[0, pl.ds(0, count), :],
            dst_ref=landed.at[later, block, pl.ds(steps, count), :],
            send_sem=part_send.at[later, 0], recv_sem=part_recv.at[later, block],
            device_id=(order[0], now), device_id_type=MESH,
        )

    for i in peers:
        arrived(0, order[i]).wait_recv()

    @pl.when(has_before)
    def _():
        for i in range(groups):
            arrived(1, order[i]).wait_recv()

    result = jnp.zeros((steps, width), F32)
    for block in range(groups):
        offset = band[me, block]
        result = result + landed[0, block, pl.ds(steps - offset, steps), :]
        result = result + landed[1, block, pl.ds(2 * steps - offset, steps), :]
    out_ref[...] = result

    for i in peers:
        place_copy(i).wait_send()
        part_copy(i, order[i], 0).wait_send()

    @pl.when(has_before)
    def _():
        edge_copy(0, now - 1).wait_send()

    @pl.when(has_after)
    def _():
        edge_copy(1, now + 1).wait_send()
        for i in range(groups):
            part_copy(i, order[i], 1).wait_send()


def solution(mesh):
    groups = mesh.shape["obs"]
    blocks = mesh.shape["tm"]

    def local(flow, point_pos, area_vec, observer_angles, band_offset):
        steps, points = flow.shape[1:]
        width = observer_angles.shape[1]
        any_spec = pl.BlockSpec(memory_space=pl.ANY)
        dma = pltpu.SemaphoreType.DMA
        return pl.pallas_call(
            functools.partial(kernel, groups, blocks),
            out_shape=jax.ShapeDtypeStruct((steps, width), F32),
            in_specs=[any_spec] * 5,
            out_specs=pl.BlockSpec(memory_space=pltpu.VMEM),
            scratch_shapes=[
                pltpu.VMEM(flow.shape, F32),
                pltpu.VMEM(point_pos.shape, F32),
                pltpu.VMEM(area_vec.shape, F32),
                pltpu.VMEM(observer_angles.shape, F32),
                pltpu.SMEM(band_offset.shape, jnp.int32),
                pltpu.VMEM((groups, 8, width), F32),
                pltpu.VMEM((2, 8, points), F32),
                pltpu.VMEM((2, 8, points), F32),
                pltpu.VMEM((4, steps, points), F32),
                pltpu.VMEM((4 * steps, 2 * points), BF16),
                pltpu.VMEM((steps, points), BF16),
                pltpu.VMEM((2, points, LAGS * width), BF16),
                pltpu.VMEM((2, 2 * points, LAGS * width), BF16),
                pltpu.VMEM((groups, steps + TAIL, width), F32),
                pltpu.VMEM((2, groups, 3 * steps, width), F32),
                dma((5,)),
                dma((groups,)),
                dma((groups,)),
                dma((2,)),
                dma((2,)),
                dma((2, groups)),
                dma((2, groups)),
            ],
            compiler_params=pltpu.CompilerParams(
                collective_id=0, has_side_effects=True, vmem_limit_bytes=40 * 1024 * 1024
            ),
        )(
            *[
                pltpu.with_memory_space_constraint(x, pltpu.HBM)
                for x in (flow, point_pos, area_vec, observer_angles, band_offset)
            ]
        )

    in_specs = (P(None, "tm", "obs"), P(None, "obs"), P(None, "obs"), P(None, "obs"), P())
    return jax.shard_map(
        local, mesh=mesh, in_specs=in_specs, out_specs=P("tm", "obs"), check_vma=False
    )
```
